512 devices in a mesh: dom: 128 (over z, y, core), feat: 4 (over x).
Axes of the slice: x: 4, y: 8, z: 8, core: 2. Of those that a mesh axis runs over, the one named last changes fastest.
Arguments:
- features: bfloat16 [256, 262144], P('feat', 'dom'), may hold values from -6 to 6
- weight: bfloat16 [256, 256], P(None, 'feat'), may hold values from -0.375 to 0.375
- cotangent: bfloat16 [256, 262144], P('feat', 'dom'), may hold values from -6 to 6
- tile_values: bfloat16 [12288, 128, 128], P('dom'), may hold values from 0 to 0.07910156
- tile_rows: int32 [12288], P('dom'), may hold values from 0 to 15
- tile_cols: int32 [12288], P('dom'), may hold values from 0 to 71
- tile_count: int32 [128], P('dom'), may hold values from 32 to 96, as said below
- send_lists: int32 [128, 7, 8], P('dom'), may hold values from 0 to 15
- send_count: int32 [128, 7], P('dom'), may hold values from 1 to 8, as said below
Outputs:
- activated: bfloat16 [256, 262144], P('feat', 'dom')
- weight_grad: float32 [256, 256], P(None, 'feat')
- feature_grad: bfloat16 [256, 262144], P('feat', 'dom')
The draws below stay inside these ranges and needn't reach their ends.
Inputs may be any that keep to these rules, and one draw needn't show every extreme that they name: `tile_count`: 96 in at least one partition. `send_count`: 8 in at least one partition in every round.
All inputs are finite; a program needn't handle non-finite values.
Results may differ from the reference program's by a relative error of at most 0.023.
Values may be sent and summed in bfloat16 or wider, within the bound.
A program may use at most 64 MiB of HBM per device.

```python
import jax
import jax.numpy as jnp
from jax import lax

H = 256
BLK = 128
NB = 16
TILES = 96
SB = 8
ROUNDS = 7
HALO = 56
NODES = 262144
TILES_ALL = 12288
N_DOM = 128


def draw_tile_count(key, part):
    key = jax.random.fold_in(key, 11)
    first, second = jax.random.split(key)
    counts = jax.random.randint(first, (N_DOM,), TILES // 3, TILES + 1)
    fullest = jax.random.randint(second, (), 0, N_DOM)
    return jnp.where(jnp.arange(N_DOM) == fullest, TILES, counts).astype(jnp.int32)


def draw_send_count(key, part):
    key = jax.random.fold_in(key, 23)
    first, second = jax.random.split(key)
    counts = jax.random.randint(first, (N_DOM, ROUNDS), 1, SB + 1)
    fullest = jax.random.randint(second, (ROUNDS,), 0, N_DOM)
    return jnp.where(jnp.arange(N_DOM)[:, None] == fullest[None, :], SB, counts).astype(jnp.int32)


def touch_ends(entries, rng, low, high):
    shape = entries.shape
    place = [jax.random.randint(jax.random.fold_in(rng, axis), (), 0, shape[axis]) for axis in range(len(shape))]
    entries = entries.at[tuple(place)].set(low)
    longest = shape.index(max(shape))
    place[longest] = (place[longest] + 1) % shape[longest]
    return entries.at[tuple(place)].set(high)


def levels(stream_key, extent, shards, least, largest):
    gain = 1.0
    for dim, blocks in shards:
        draws = jax.random.uniform(jax.random.fold_in(jax.random.fold_in(stream_key, 6), dim), (blocks,), jnp.float32, least / len(shards), largest / len(shards))
        gain = gain * jnp.repeat(jnp.exp(draws), extent[dim] // blocks).reshape((-1,) + (1,) * (len(extent) - 1 - dim))
    return gain


def scatter_about(own_key, shape, width, reach, shards=(), held_as=jnp.bfloat16):
    entries = jax.random.normal(own_key, shape, jnp.float32) * width
    if len(shards) > 0:
        entries = levels(own_key, shape, shards, -0.22, 0.18) * entries
    return jnp.clip(entries, min=-reach, max=reach).astype(held_as)


def setup_inputs(seed: int = 0) -> dict:
    splits = jax.random.split(jax.random.key(seed), 10)
    return {
        "features": scatter_about(splits[0], (H, NODES), 1.0, 6.0, ((0, 4), (1, 128))),
        "weight": scatter_about(splits[1], (H, H), H ** -0.5, 0.375, ((1, 4),)),
        "cotangent": scatter_about(splits[2], (H, NODES), 1.0, 6.0, ((0, 4), (1, 128))),
        "tile_values": jnp.clip(0.07910156 * jax.random.uniform(splits[3], (TILES_ALL, BLK, BLK), jnp.float32) ** levels(splits[3], (TILES_ALL, BLK, BLK), ((0, 128),), -0.2, 0.2), 0.0, 0.07910156).astype(jnp.bfloat16),
        "tile_rows": touch_ends(jax.random.randint(splits[4], (TILES_ALL,), 0, NB), jax.random.fold_in(splits[4], 1), 0, NB - 1).astype(jnp.int32),
        "tile_cols": touch_ends(jax.random.randint(splits[5], (TILES_ALL,), 0, NB + HALO), jax.random.fold_in(splits[5], 1), 0, (NB + HALO) - 1).astype(jnp.int32),
        "tile_count": draw_tile_count(jax.random.fold_in(splits[9], 71), 0),
        "send_lists": touch_ends(jax.random.randint(splits[7], (N_DOM, ROUNDS, SB), 0, NB), jax.random.fold_in(splits[7], 1), 0, NB - 1).astype(jnp.int32),
        "send_count": draw_send_count(jax.random.fold_in(splits[9], 71), 0),
    }


def gelu_tanh(values):
    return jax.nn.gelu(values, approximate=True)

def gelu_backward(pre, upstream):
    return jax.vjp(gelu_tanh, pre)[1](upstream)[0]

def reference(features, weight, cotangent, tile_values, tile_rows, tile_cols, tile_count, send_lists, send_count):
    feature_blocks = features.reshape(H, N_DOM, NB, BLK)
    tiles_all = tile_values.reshape(N_DOM, TILES, BLK, BLK)
    rows_all = tile_rows.reshape(N_DOM, TILES)
    cols_all = tile_cols.reshape(N_DOM, TILES)
    slot_range = jnp.arange(SB, dtype=jnp.int32)
    tile_range = jnp.arange(TILES, dtype=jnp.int32)
    highest = lax.Precision.HIGHEST

    def boundary_of(part_index):
        pieces = []
        for level in range(ROUNDS):
            partner = jnp.bitwise_xor(part_index, jnp.int32(1 << level))
            chosen = jnp.take(feature_blocks[:, partner], send_lists[partner, level], axis=1)
            keep = (slot_range < send_count[partner, level]).astype(jnp.bfloat16)
            pieces.append(chosen * keep[None, :, None])
        return jnp.concatenate(pieces, axis=1)

    def forward_part(part_index):
        sources = jnp.concatenate([feature_blocks[:, part_index], boundary_of(part_index)], axis=1)
        live = (tile_range < tile_count[part_index]).astype(jnp.float32)
        picked = jnp.take(sources, cols_all[part_index], axis=1).astype(jnp.float32)
        contrib = jnp.einsum('ftc,trc->ftr', picked, tiles_all[part_index].astype(jnp.float32), precision=highest)
        onehot = (rows_all[part_index][:, None] == jnp.arange(NB, dtype=jnp.int32)[None, :]).astype(jnp.float32) * live[:, None]
        return jnp.einsum('ftr,tk->fkr', contrib, onehot, precision=highest).astype(jnp.bfloat16)
    part_range = jnp.arange(N_DOM, dtype=jnp.int32)
    aggregated = lax.map(forward_part, part_range).transpose(1, 0, 2, 3).reshape(H, NODES)
    pre = jnp.dot(weight.T, aggregated, preferred_element_type=jnp.float32)
    activated = gelu_tanh(pre).astype(jnp.bfloat16)
    pre_grad = gelu_backward(pre, cotangent.astype(jnp.float32)).astype(jnp.bfloat16)
    weight_grad = jnp.dot(aggregated, pre_grad.T, preferred_element_type=jnp.float32) / jnp.sqrt(jnp.float32(NODES))
    agg_grad = jnp.dot(weight, pre_grad, preferred_element_type=jnp.float32).astype(jnp.bfloat16)
    grad_blocks = agg_grad.reshape(H, N_DOM, NB, BLK)

    def backward_part(part_index):
        live = (tile_range < tile_count[part_index]).astype(jnp.float32)
        picked = jnp.take(grad_blocks[:, part_index], rows_all[part_index], axis=1).astype(jnp.float32)
        contrib = jnp.einsum('ftr,trc->ftc', picked, tiles_all[part_index].astype(jnp.float32), precision=highest)
        onehot = (cols_all[part_index][:, None] == jnp.arange(NB + HALO, dtype=jnp.int32)[None, :]).astype(jnp.float32) * live[:, None]
        return jnp.einsum('ftc,ts->fsc', contrib, onehot, precision=highest)
    source_grads = lax.map(backward_part, part_range)

    def collect_part(part_index):
        total = source_grads[part_index][:, :NB]
        for level in range(ROUNDS):
            partner = jnp.bitwise_xor(part_index, jnp.int32(1 << level))
            returned = source_grads[partner][:, NB + level * SB:NB + (level + 1) * SB]
            keep = (slot_range < send_count[part_index, level]).astype(jnp.float32)
            onehot = (send_lists[part_index, level][:, None] == jnp.arange(NB, dtype=jnp.int32)[None, :]).astype(jnp.float32) * keep[:, None]
            total = total + jnp.einsum('fjc,jk->fkc', returned, onehot, precision=highest)
        return total.astype(jnp.bfloat16)
    feature_grad = lax.map(collect_part, part_range).transpose(1, 0, 2, 3).reshape(H, NODES)
    return (activated, weight_grad, feature_grad)
```

```python
import functools

import jax
import jax.numpy as jnp
from jax import lax
from jax.experimental import pallas as pl
from jax.experimental.pallas import tpu as pltpu
from jax.sharding import PartitionSpec as P

MESH = pl.DeviceIdType.MESH
CHUNKS = 2
UNROLL = 8
LANES = 128
GELU_C = 0.7978845608028654
GELU_A = 0.044715
F_PERM, F_SRC, F_KEEP, F_LAST, F_HAS = 0, 1, 2, 3, 4
B_PERM, B_SRC, B_KEEP, B_LAST, B_HAS = 5, 6, 7, 8, 9
E_PERM, E_KEEP, E_LAST, E_HAS = 10, 11, 12, 13


def sorted_order(key_row, other_row):
    shape = (LANES, LANES)
    ii = lax.broadcasted_iota(jnp.int32, shape, 0)
    jj = lax.broadcasted_iota(jnp.int32, shape, 1)
    key_l = jnp.broadcast_to(key_row, shape)
    other_l = jnp.broadcast_to(other_row, shape)
    key_s = jnp.sum(jnp.where(ii == jj, key_l, 0), axis=1, keepdims=True)
    other_s = jnp.sum(jnp.where(ii == jj, other_l, 0), axis=1, keepdims=True)
    same = jnp.where((key_l == key_s) & (jj < ii), 1, 0)
    dup_s = jnp.sum(same, axis=1, keepdims=True)
    rank_s = dup_s + jnp.sum(jnp.where(key_l < key_s, 1, 0), axis=1, keepdims=True)
    place = rank_s == jj
    perm = jnp.sum(jnp.where(place, ii, 0), axis=0, keepdims=True)
    other = jnp.sum(jnp.where(place, other_s, 0), axis=0, keepdims=True)
    keep = jnp.sum(jnp.where(place, jnp.minimum(dup_s, 1), 0), axis=0, keepdims=True)
    last = jnp.sum(jnp.where(key_s <= jj, 1, 0), axis=0, keepdims=True) - 1
    has = jnp.sum(jnp.where(key_s == jj, 1, 0), axis=0, keepdims=True)
    return perm, other, keep, jnp.maximum(last, 0), jnp.minimum(has, 1)


def kernel(
    cfg,
    x_hbm, w_hbm, cot_hbm, tiles_hbm, rows_s, cols_s, count_s, lists_s, sc_s,
    act_hbm, wgrad_ref, fg_hbm,
    *scratch,
):
    (H, FR, NODES, NB, T, R, SB, D, F, PLANE, Z) = cfg
    C = CHUNKS
    ROWS = FR // C
    HALO = R * SB
    NBQ = NB // F
    NQ = NODES // F
    refs = list(scratch)

    def take(n):
        out = refs[:n]
        del refs[:n]
        return out

    (xv, xb, tv, snd, aggS, aggG, cotG, wg, wfull, wt, pg, actS, agS) = take(13)
    src = take(C)
    gb = take(C)
    (buf, ret_s) = take(2)
    ret_r = take(C)
    (ebuf, fgv, wpS, wxR, wR, rsR, zR, finR, tab_v, tab_s) = take(10)
    (loc_sem, halo_sem, a2a_sem, w_sem, cot_sem, act_sem, ag_sem, ret_sem, wx_sem, rs_sem, z_sem, fin_sem) = take(12)

    dom = lax.axis_index("dom")
    me = lax.axis_index("feat")
    m = lax.rem(dom, PLANE)
    zi = dom // PLANE

    def dom_at(mm, zz):
        return zz * PLANE + mm

    barrier = pltpu.get_barrier_semaphore()
    for d in range(1, F):
        pl.semaphore_signal(barrier, inc=1, device_id=(dom, lax.rem(me + d, F)), device_id_type=MESH)

    def hello_plane(d, c):
        pl.semaphore_signal(
            barrier, inc=1, device_id=(dom_at(lax.rem(m + d, PLANE), zi), me), device_id_type=MESH
        )
        return c

    lax.fori_loop(1, PLANE, hello_plane, 0)

    def hello_z(d, c):
        pl.semaphore_signal(
            barrier, inc=1, device_id=(dom_at(m, lax.rem(zi + d, Z)), me), device_id_type=MESH
        )
        return c

    lax.fori_loop(1, Z, hello_z, 0)

    load_x = pltpu.make_async_copy(x_hbm, xv, loc_sem.at[0])
    load_x.start()
    load_t = pltpu.make_async_copy(tiles_hbm, tv, loc_sem.at[1])
    load_t.start()
    own_cot = pltpu.make_async_copy(
        cot_hbm.at[:, pl.ds(pl.multiple_of(me * NQ, LANES), NQ)],
        cotG.at[pl.ds(pl.multiple_of(me * FR, 16), FR), :],
        loc_sem.at[2],
    )
    own_cot.start()
    own_w = pltpu.make_async_copy(w_hbm, wg.at[me], loc_sem.at[3])
    own_w.start()
    load_x.wait()

    for k in range(NB):
        xb[k] = xv[:, k * LANES : (k + 1) * LANES]
    zero_block = jnp.zeros((FR, LANES), jnp.int32)
    for b in range(R):

        def fill(j, c, b=b):
            live = (zero_block + j < sc_s[0, b]).astype(jnp.float32)
            block = (xb[lists_s[0, b, j]].astype(jnp.float32) * live).astype(jnp.bfloat16)
            for h in range(C):
                snd[h, b * SB + j] = block[h * ROWS : (h + 1) * ROWS]
            return c

        lax.fori_loop(0, SB, fill, 0)

    pl.semaphore_wait(barrier, (F - 1) + (PLANE - 1) + (Z - 1))

    def halo_copy(h, b):
        return pltpu.make_async_remote_copy(
            src_ref=snd.at[h, pl.ds(b * SB, SB)],
            dst_ref=src[h].at[pl.ds(NB + b * SB, SB)],
            send_sem=halo_sem.at[0, h * R + b],
            recv_sem=halo_sem.at[1, h * R + b],
            device_id=(partner(b), me),
            device_id_type=MESH,
        )

    def partner(b):
        step = 1 << b
        bit = lax.rem(dom // step, 2)
        return dom + step - 2 * step * bit

    def feat_peer(d):
        return lax.rem(me + d, F)

    order = list(range(R))[::-1]
    sends = []
    halo = {}
    for b in order:
        halo[0, b] = halo_copy(0, b)
        halo[0, b].start()
    w_copies, cot_copies = [], []
    for d in range(1, F):
        q = feat_peer(d)
        cp = pltpu.make_async_remote_copy(
            src_ref=w_hbm,
            dst_ref=wg.at[me],
            send_sem=w_sem.at[0, d],
            recv_sem=w_sem.at[1, d],
            device_id=(dom, q),
            device_id_type=MESH,
        )
        cp.start()
        w_copies.append(cp)
        cp = pltpu.make_async_remote_copy(
            src_ref=cot_hbm.at[:, pl.ds(pl.multiple_of(q * NQ, LANES), NQ)],
            dst_ref=cotG.at[pl.ds(pl.multiple_of(me * FR, 16), FR), :],
            send_sem=cot_sem.at[0, d],
            recv_sem=cot_sem.at[1, d],
            device_id=(dom, q),
            device_id_type=MESH,
        )
        cp.start()
        cot_copies.append(cp)
    for h in range(1, C):
        for b in order:
            halo[h, b] = halo_copy(h, b)
            halo[h, b].start()

    lane = lax.broadcasted_iota(jnp.int32, (1, LANES), 1)

    def read_tile(t, c):
        r, k = c
        return jnp.where(lane == t, rows_s[t], r), jnp.where(lane == t, cols_s[t], k)

    zero_row = jnp.zeros((1, LANES), jnp.int32)
    rows_v, cols_v = lax.fori_loop(0, T, read_tile, (zero_row, zero_row))

    list_v = zero_row + (LANES - 1)
    for b in range(R):

        def read_entry(j, c, b=b):
            return jnp.where((lane == b * SB + j) & (zero_row + j < sc_s[0, b]), lists_s[0, b, j], c)

        list_v = lax.fori_loop(0, SB, read_entry, list_v)
    dead = lane >= count_s[0]
    fwd = sorted_order(jnp.where(dead, LANES - 1, rows_v), cols_v)
    bwd = sorted_order(jnp.where(dead, LANES - 1, cols_v), rows_v)
    ent = sorted_order(list_v, list_v)
    for place, row in zip(
        (F_PERM, F_SRC, F_KEEP, F_LAST, F_HAS, B_PERM, B_SRC, B_KEEP, B_LAST, B_HAS, E_PERM, E_KEEP, E_LAST, E_HAS),
        fwd + bwd + (ent[0],) + ent[2:],
    ):
        tab_v[pl.ds(place, 1), :] = row
    tab_v[pl.ds(14, 2), :] = jnp.zeros((2, LANES), jnp.int32)
    table = pltpu.make_async_copy(tab_v, tab_s, loc_sem.at[4])
    table.start()

    for k in range(NB):
        for h in range(C):
            src[h][k] = xb[k, h * ROWS : (h + 1) * ROWS]

    own_w.wait()
    for cp in w_copies:
        cp.wait_recv()
    wall = jnp.concatenate([wg[q].astype(jnp.float32) for q in range(F)], axis=1)
    wfull[...] = wall.astype(jnp.bfloat16)
    wt[...] = jnp.transpose(wall).astype(jnp.bfloat16)

    table.wait()
    load_t.wait()

    def tile_pass(source, perm, other, keep, contract):
        def body(i, run):
            for u in range(UNROLL):
                t = i * UNROLL + u
                part = lax.dot_general(
                    source[tab_s[other, t]],
                    tv[tab_s[perm, t]],
                    (((1,), (contract,)), ((), ())),
                    preferred_element_type=jnp.float32,
                )
                run = run * tab_s[keep, t].astype(jnp.float32) + part
                buf[t] = run
            return run

        lax.fori_loop(0, T // UNROLL, body, jnp.zeros((ROWS, LANES), jnp.float32))

    def segment(values, last, has, k):
        return values[tab_s[last, k]] * tab_s[has, k].astype(jnp.float32)

    a2a, a2a_own = [], []
    for h in range(C):
        for b in order:
            halo[h, b].wait_recv()
        tile_pass(src[h], F_PERM, F_SRC, F_KEEP, 1)
        for k in range(NB):
            aggS[h, k // NBQ, :, (k % NBQ) * LANES : (k % NBQ + 1) * LANES] = segment(
                buf, F_LAST, F_HAS, k
            ).astype(jnp.bfloat16)
        place = pl.ds(pl.multiple_of(me * FR + h * ROWS, 16), ROWS)
        for d in range(1, F):
            q = feat_peer(d)
            cp = pltpu.make_async_remote_copy(
                src_ref=aggS.at[h, q],
                dst_ref=aggG.at[place, :],
                send_sem=a2a_sem.at[0, h * F + d],
                recv_sem=a2a_sem.at[1, h * F + d],
                device_id=(dom, q),
                device_id_type=MESH,
            )
            cp.start()
            a2a.append(cp)
        cp = pltpu.make_async_copy(aggS.at[h, me], aggG.at[place, :], loc_sem.at[5 + h])
        cp.start()
        a2a_own.append(cp)

    own_cot.wait()
    for cp in cot_copies:
        cp.wait_recv()
    for cp in a2a_own:
        cp.wait()
    for cp in a2a:
        cp.wait_recv()

    def dense(q, c):
        here = pl.ds(pl.multiple_of(q * FR, 16), FR)
        pre = jnp.dot(wt[here, :], aggG[...], preferred_element_type=jnp.float32)
        square = pre * pre
        t = jnp.tanh(GELU_C * pre * (1.0 + GELU_A * square))
        half = 0.5 * (1.0 + t)
        actS[q] = (pre * half).astype(jnp.bfloat16)
        slope = half + (0.5 * GELU_C) * pre * (1.0 - t * t) * (1.0 + (3.0 * GELU_A) * square)
        pg[here, :] = (cotG[here, :].astype(jnp.float32) * slope).astype(jnp.bfloat16)
        return c

    lax.fori_loop(0, F, dense, 0)

    ag, ag_own = [], []
    for h in range(C):

        def agg_grad(q, c, h=h):
            here = pl.ds(pl.multiple_of(q * FR + h * ROWS, 16), ROWS)
            g = jnp.dot(wfull[here, :], pg[...], preferred_element_type=jnp.float32).astype(jnp.bfloat16)
            for k in range(NBQ):
                agS[h, q, k] = g[:, k * LANES : (k + 1) * LANES]
            return c

        lax.fori_loop(0, F, agg_grad, 0)
        place = pl.ds(me * NBQ, NBQ)
        for d in range(1, F):
            q = feat_peer(d)
            cp = pltpu.make_async_remote_copy(
                src_ref=agS.at[h, q],
                dst_ref=gb[h].at[place],
                send_sem=ag_sem.at[0, h * F + d],
                recv_sem=ag_sem.at[1, h * F + d],
                device_id=(dom, q),
                device_id_type=MESH,
            )
            cp.start()
            ag.append(cp)
        cp = pltpu.make_async_copy(agS.at[h, me], gb[h].at[place], loc_sem.at[5 + C + h])
        cp.start()
        ag_own.append(cp)

    place = pl.ds(pl.multiple_of(me * NQ, LANES), NQ)
    act = []
    for d in range(1, F):
        q = feat_peer(d)
        cp = pltpu.make_async_remote_copy(
            src_ref=actS.at[q],
            dst_ref=act_hbm.at[:, place],
            send_sem=act_sem.at[0, d],
            recv_sem=act_sem.at[1, d],
            device_id=(dom, q),
            device_id_type=MESH,
        )
        cp.start()
        act.append(cp)
    act_own = pltpu.make_async_copy(actS.at[me], act_hbm.at[:, place], loc_sem.at[5 + 2 * C])
    act_own.start()

    def weight_term(q, c):
        here = pl.ds(pl.multiple_of(q * FR, 16), FR)
        wpS[q] = lax.dot_general(
            pg[here, :], aggG[...], (((1,), (1,)), ((), ())), preferred_element_type=jnp.float32
        )
        return c

    lax.fori_loop(0, F, weight_term, 0)
    wx = []
    for d in range(1, F):
        cp = pltpu.make_async_remote_copy(
            src_ref=wpS.at[feat_peer(d)],
            dst_ref=wxR.at[d],
            send_sem=wx_sem.at[0, d],
            recv_sem=wx_sem.at[1, d],
            device_id=(dom, feat_peer(d)),
            device_id_type=MESH,
        )
        cp.start()
        wx.append(cp)

    def plane_copy(d, from_ref, to_ref, sem):
        mm = lax.rem(m + d, PLANE)
        return pltpu.make_async_remote_copy(
            src_ref=from_ref(mm),
            dst_ref=to_ref.at[m],
            send_sem=sem.at[0, d],
            recv_sem=sem.at[1, d],
            device_id=(dom_at(mm, zi), me),
            device_id_type=MESH,
        )

    def rs_copy(d):
        return plane_copy(d, lambda mm: wR.at[mm], rsR, rs_sem)

    def fin_copy(d):
        return plane_copy(d, lambda mm: finR.at[m], finR, fin_sem)

    def z_copy(d):
        return pltpu.make_async_remote_copy(
            src_ref=zR.at[zi],
            dst_ref=zR.at[zi],
            send_sem=z_sem.at[0, d],
            recv_sem=z_sem.at[1, d],
            device_id=(dom_at(m, lax.rem(zi + d, Z)), me),
            device_id_type=MESH,
        )

    def each(low, high, act_on):
        def body(d, c):
            act_on(d)
            return c

        lax.fori_loop(low, high, body, 0)

    across = H // LANES

    def reduce_feat():
        for cp in wx:
            cp.wait_recv()
        total = wpS[me]
        for d in range(1, F):
            total = total + wxR[d]
        for p in range(PLANE):
            wR[p] = total[8 * (p // across) : 8 * (p // across) + 8, LANES * (p % across) : LANES * (p % across + 1)]
        each(1, PLANE, lambda d: rs_copy(d).start())

    def reduce_plane():
        rsR[m] = wR[m]
        each(1, PLANE, lambda d: rs_copy(d).wait_recv())
        total = rsR[0]
        for p in range(1, PLANE):
            total = total + rsR[p]
        zR[zi] = total
        each(1, Z, lambda d: z_copy(d).start())

    def reduce_z():
        each(1, Z, lambda d: z_copy(d).wait_recv())
        total = zR[0]
        for p in range(1, Z):
            total = total + zR[p]
        finR[m] = total * (float(NODES * D) ** -0.5)
        each(1, PLANE, lambda d: fin_copy(d).start())

    def finish_weight():
        each(1, PLANE, lambda d: fin_copy(d).wait_recv())
        whole = jnp.concatenate(
            [
                jnp.concatenate([finR[r * across + a] for a in range(across)], axis=1)
                for r in range(FR // 8)
            ],
            axis=0,
        )
        wgrad_ref[...] = jnp.transpose(whole)

    def ret_copy(h, b):
        return pltpu.make_async_remote_copy(
            src_ref=ret_s.at[h, pl.ds(b * SB, SB)],
            dst_ref=ret_r[h].at[pl.ds(b * SB, SB)],
            send_sem=ret_sem.at[0, h * R + b],
            recv_sem=ret_sem.at[1, h * R + b],
            device_id=(partner(b), me),
            device_id_type=MESH,
        )

    ret = {}
    for h in range(C):
        ag_own[h].wait()
        for cp in ag[h * (F - 1) : (h + 1) * (F - 1)]:
            cp.wait_recv()
        tile_pass(gb[h], B_PERM, B_SRC, B_KEEP, 0)
        for b in order:
            for j in range(SB):
                s = b * SB + j
                ret_s[h, s] = segment(buf, B_LAST, B_HAS, NB + s).astype(jnp.bfloat16)
            ret[h, b] = ret_copy(h, b)
            ret[h, b].start()
        for k in range(NB):
            fgv[h, k] = segment(buf, B_LAST, B_HAS, k)
        if h == 0:
            reduce_feat()
    reduce_plane()

    outs = []
    for h in range(C):
        for b in order:
            ret[h, b].wait_recv()

        def gather_entry(e, run, h=h):
            run = run * tab_s[E_KEEP, e].astype(jnp.float32) + ret_r[h][tab_s[E_PERM, e]].astype(jnp.float32)
            ebuf[e] = run
            return run

        lax.fori_loop(0, HALO, gather_entry, jnp.zeros((ROWS, LANES), jnp.float32))
        for k in range(NB):
            xv[h * ROWS : (h + 1) * ROWS, k * LANES : (k + 1) * LANES] = (
                fgv[h, k] + segment(ebuf, E_LAST, E_HAS, k)
            ).astype(jnp.bfloat16)
        here = pl.ds(h * ROWS, ROWS)
        cp = pltpu.make_async_copy(xv.at[here, :], fg_hbm.at[here, :], loc_sem.at[6 + 2 * C + h])
        cp.start()
        outs.append(cp)
        if h == 0:
            reduce_z()
    finish_weight()

    for cp in outs:
        cp.wait()
    act_own.wait()
    for cp in act:
        cp.wait_recv()
    for cp in list(halo.values()) + w_copies + cot_copies + a2a + ag + act + wx + list(ret.values()):
        cp.wait_send()
    each(1, PLANE, lambda d: rs_copy(d).wait_send())
    each(1, Z, lambda d: z_copy(d).wait_send())
    each(1, PLANE, lambda d: fin_copy(d).wait_send())


def local(D, F, features, weight, cotangent, tile_values, tile_rows, tile_cols, tile_count, send_lists, send_count):
    FR, NODES = features.shape
    H = weight.shape[0]
    T, BLK, _ = tile_values.shape
    NB = NODES // BLK
    _, R, SB = send_lists.shape
    PLANE = min(D, FR * H // 1024)
    Z = D // PLANE
    C = CHUNKS
    ROWS = FR // C
    HALO = R * SB
    NBQ, NQ = NB // F, NODES // F
    cfg = (H, FR, NODES, NB, T, R, SB, D, F, PLANE, Z)
    bf, f32 = jnp.bfloat16, jnp.float32
    V = pltpu.VMEM
    scratch = [
        V((FR, NODES), bf),
        V((NB, FR, BLK), bf),
        V((T, BLK, BLK), bf),
        V((C, HALO, ROWS, BLK), bf),
        V((C, F, ROWS, NQ), bf),
        V((H, NQ), bf),
        V((H, NQ), bf),
        V((F, H, FR), bf),
        V((H, H), bf),
        V((H, H), bf),
        V((H, NQ), bf),
        V((F, FR, NQ), bf),
        V((C, F, NBQ, ROWS, BLK), bf),
    ]
    scratch += [V((NB + HALO, ROWS, BLK), bf) for _ in range(C)]
    scratch += [V((NB, ROWS, BLK), bf) for _ in range(C)]
    scratch += [V((T, ROWS, BLK), f32), V((C, HALO, ROWS, BLK), bf)]
    scratch += [V((HALO, ROWS, BLK), bf) for _ in range(C)]
    scratch += [
        V((HALO, ROWS, BLK), f32),
        V((C, NB, ROWS, BLK), f32),
        V((F, FR, H), f32),
        V((F, FR, H), f32),
        V((PLANE, 8, LANES), f32),
        V((PLANE, 8, LANES), f32),
        V((Z, 8, LANES), f32),
        V((PLANE, 8, LANES), f32),
        V((16, LANES), jnp.int32),
        pltpu.SMEM((16, LANES), jnp.int32),
    ]
    sem = pltpu.SemaphoreType.DMA
    scratch += [
        sem((6 + 3 * C,)),
        sem((2, C * R)),
        sem((2, C * F)),
        sem((2, F)),
        sem((2, F)),
        sem((2, F)),
        sem((2, C * F)),
        sem((2, C * R)),
        sem((2, F)),
        sem((2, PLANE)),
        sem((2, Z)),
        sem((2, PLANE)),
    ]
    any_spec = pl.BlockSpec(memory_space=pl.ANY)
    smem = pl.BlockSpec(memory_space=pltpu.SMEM)
    return pl.pallas_call(
        functools.partial(kernel, cfg),
        out_shape=(
            jax.ShapeDtypeStruct((FR, NODES), bf),
            jax.ShapeDtypeStruct((H, FR), f32),
            jax.ShapeDtypeStruct((FR, NODES), bf),
        ),
        in_specs=[any_spec] * 4 + [smem] * 5,
        out_specs=(any_spec, pl.BlockSpec(memory_space=pltpu.VMEM), any_spec),
        scratch_shapes=scratch,
        compiler_params=pltpu.CompilerParams(
            collective_id=0, has_side_effects=True, vmem_limit_bytes=48 * 1024 * 1024
        ),
    )(features, weight, cotangent, tile_values, tile_rows, tile_cols, tile_count, send_lists, send_count)


def solution(mesh):
    return jax.shard_map(
        functools.partial(local, mesh.shape["dom"], mesh.shape["feat"]),
        mesh=mesh,
        in_specs=(
            P("feat", "dom"),
            P(None, "feat"),
            P("feat", "dom"),
            P("dom", None, None),
            P("dom"),
            P("dom"),
            P("dom"),
            P("dom", None, None),
            P("dom", None),
        ),
        out_specs=(P("feat", "dom"), P(None, "feat"), P("feat", "dom")),
        check_vma=False,
    )
```

```python
import functools

import jax
import jax.numpy as jnp
from jax import lax
from jax.experimental import pallas as pl
from jax.experimental.pallas import tpu as pltpu
from jax.sharding import PartitionSpec as P

MESH = pl.DeviceIdType.MESH
CHUNKS = 2
UNROLL = 8
LANES = 128
VMEM_LIMIT = 63 * 1024 * 1024
GELU_C = 0.7978845608028654
GELU_A = 0.044715
F_PERM, F_SRC, F_KEEP, F_LAST, F_HAS = 0, 1, 2, 3, 4
B_PERM, B_SRC, B_KEEP, B_LAST, B_HAS = 5, 6, 7, 8, 9
E_PERM, E_KEEP, E_LAST, E_HAS = 10, 11, 12, 13


def sorted_order(key_row, other_row):
    shape = (LANES, LANES)
    ii = lax.broadcasted_iota(jnp.int32, shape, 0)
    jj = lax.broadcasted_iota(jnp.int32, shape, 1)
    key_l = jnp.broadcast_to(key_row, shape)
    other_l = jnp.broadcast_to(other_row, shape)
    key_s = jnp.sum(jnp.where(ii == jj, key_l, 0), axis=1, keepdims=True)
    other_s = jnp.sum(jnp.where(ii == jj, other_l, 0), axis=1, keepdims=True)
    same = jnp.where((key_l == key_s) & (jj < ii), 1, 0)
    dup_s = jnp.sum(same, axis=1, keepdims=True)
    rank_s = dup_s + jnp.sum(jnp.where(key_l < key_s, 1, 0), axis=1, keepdims=True)
    place = rank_s == jj
    perm = jnp.sum(jnp.where(place, ii, 0), axis=0, keepdims=True)
    other = jnp.sum(jnp.where(place, other_s, 0), axis=0, keepdims=True)
    keep = jnp.sum(jnp.where(place, jnp.minimum(dup_s, 1), 0), axis=0, keepdims=True)
    last = jnp.sum(jnp.where(key_s <= jj, 1, 0), axis=0, keepdims=True) - 1
    has = jnp.sum(jnp.where(key_s == jj, 1, 0), axis=0, keepdims=True)
    return perm, other, keep, jnp.maximum(last, 0), jnp.minimum(has, 1)


def kernel(
    cfg,
    x_hbm, w_hbm, cot_hbm, tiles_hbm, rows_hbm, cols_hbm, count_hbm, lists_hbm, sc_hbm,
    act_hbm, wgrad_hbm, fg_hbm,
    *scratch,
):
    (H, FR, NODES, NB, T, R, SB, D, F, PLANE, Z) = cfg
    C = CHUNKS
    ROWS = FR // C
    HALO = R * SB
    NBQ = NB // F
    NQ = NODES // F
    refs = list(scratch)

    def take(n):
        out = refs[:n]
        del refs[:n]
        return out

    (xv, xb, tv, snd, aggS, aggG, cotG, wfull, wt, pg, actS, agS) = take(12)
    src = take(C)
    gb = take(C)
    (buf, ret_s) = take(2)
    ret_r = take(C)
    (ebuf, fgv, wpS, wxR, wR, rsR, zR, finR, wgv, tab_v, tab_s) = take(11)
    (rows_s, cols_s, count_s, lists_s, sc_s) = take(5)
    (in_sem, loc_sem, halo_sem, a2a_sem, w_sem, cot_sem, act_sem, ag_sem, ret_sem, wx_sem, rs_sem, z_sem, fin_sem) = take(13)

    dom = lax.axis_index("dom")
    me = lax.axis_index("feat")
    m = lax.rem(dom, PLANE)
    zi = dom // PLANE

    def dom_at(mm, zz):
        return zz * PLANE + mm

    barrier = pltpu.get_barrier_semaphore()
    for d in range(1, F):
        pl.semaphore_signal(barrier, inc=1, device_id=(dom, lax.rem(me + d, F)), device_id_type=MESH)

    def hello_plane(d, c):
        pl.semaphore_signal(
            barrier, inc=1, device_id=(dom_at(lax.rem(m + d, PLANE), zi), me), device_id_type=MESH
        )
        return c

    lax.fori_loop(1, PLANE, hello_plane, 0)

    def hello_z(d, c):
        pl.semaphore_signal(
            barrier, inc=1, device_id=(dom_at(m, lax.rem(zi + d, Z)), me), device_id_type=MESH
        )
        return c

    lax.fori_loop(1, Z, hello_z, 0)

    small = []
    for i, (a, b) in enumerate(
        ((lists_hbm, lists_s), (sc_hbm, sc_s), (rows_hbm, rows_s), (cols_hbm, cols_s), (count_hbm, count_s))
    ):
        small.append(pltpu.make_async_copy(a, b, in_sem.at[i]))
        small[-1].start()
    load_x = pltpu.make_async_copy(x_hbm, xv, loc_sem.at[0])
    load_x.start()
    load_t = pltpu.make_async_copy(tiles_hbm, tv, loc_sem.at[1])
    load_t.start()
    own_cot = pltpu.make_async_copy(
        cot_hbm.at[:, pl.ds(pl.multiple_of(me * NQ, LANES), NQ)],
        cotG.at[pl.ds(pl.multiple_of(me * FR, 16), FR), :],
        loc_sem.at[2],
    )
    own_cot.start()
    own_rows = pl.ds(pl.multiple_of(me * FR, 16), FR)
    own_w = pltpu.make_async_copy(w_hbm, wt.at[own_rows, :], loc_sem.at[3])
    own_w.start()
    load_x.wait()
    for cp in small:
        cp.wait()

    for k in range(NB):
        xb[k] = xv[:, k * LANES : (k + 1) * LANES]
    zero_block = jnp.zeros((FR, LANES), jnp.int32)
    for b in range(R):

        def fill(j, c, b=b):
            live = (zero_block + j < sc_s[0, b]).astype(jnp.float32)
            block = (xb[lists_s[b, 0, j]].astype(jnp.float32) * live).astype(jnp.bfloat16)
            for h in range(C):
                snd[h, b * SB + j] = block[h * ROWS : (h + 1) * ROWS]
            return c

        lax.fori_loop(0, SB, fill, 0)

    pl.semaphore_wait(barrier, (F - 1) + (PLANE - 1) + (Z - 1))

    def halo_copy(h, b):
        return pltpu.make_async_remote_copy(
            src_ref=snd.at[h, pl.ds(b * SB, SB)],
            dst_ref=src[h].at[pl.ds(NB + b * SB, SB)],
            send_sem=halo_sem.at[0, h * R + b],
            recv_sem=halo_sem.at[1, h * R + b],
            device_id=(partner(b), me),
            device_id_type=MESH,
        )

    def partner(b):
        step = 1 << b
        bit = lax.rem(dom // step, 2)
        return dom + step - 2 * step * bit

    def feat_peer(d):
        return lax.rem(me + d, F)

    order = list(range(R))[::-1]
    sends = []
    halo = {}
    for b in order:
        halo[0, b] = halo_copy(0, b)
        halo[0, b].start()
    w_copies, cot_copies = [], []
    for d in range(1, F):
        q = feat_peer(d)
        cp = pltpu.make_async_remote_copy(
            src_ref=w_hbm,
            dst_ref=wt.at[own_rows, :],
            send_sem=w_sem.at[0, d],
            recv_sem=w_sem.at[1, d],
            device_id=(dom, q),
            device_id_type=MESH,
        )
        cp.start()
        w_copies.append(cp)
        cp = pltpu.make_async_remote_copy(
            src_ref=cot_hbm.at[:, pl.ds(pl.multiple_of(q * NQ, LANES), NQ)],
            dst_ref=cotG.at[pl.ds(pl.multiple_of(me * FR, 16), FR), :],
            send_sem=cot_sem.at[0, d],
            recv_sem=cot_sem.at[1, d],
            device_id=(dom, q),
            device_id_type=MESH,
        )
        cp.start()
        cot_copies.append(cp)
    for h in range(1, C):
        for b in order:
            halo[h, b] = halo_copy(h, b)
            halo[h, b].start()

    lane = lax.broadcasted_iota(jnp.int32, (1, LANES), 1)

    def read_tile(t, c):
        r, k = c
        return jnp.where(lane == t, rows_s[t], r), jnp.where(lane == t, cols_s[t], k)

    zero_row = jnp.zeros((1, LANES), jnp.int32)
    rows_v, cols_v = lax.fori_loop(0, T, read_tile, (zero_row, zero_row))

    list_v = zero_row + (LANES - 1)
    for b in range(R):

        def read_entry(j, c, b=b):
            return jnp.where((lane == b * SB + j) & (zero_row + j < sc_s[0, b]), lists_s[b, 0, j], c)

        list_v = lax.fori_loop(0, SB, read_entry, list_v)
    dead = lane >= count_s[0]
    fwd = sorted_order(jnp.where(dead, LANES - 1, rows_v), cols_v)
    bwd = sorted_order(jnp.where(dead, LANES - 1, cols_v), rows_v)
    ent = sorted_order(list_v, list_v)
    for place, row in zip(
        (F_PERM, F_SRC, F_KEEP, F_LAST, F_HAS, B_PERM, B_SRC, B_KEEP, B_LAST, B_HAS, E_PERM, E_KEEP, E_LAST, E_HAS),
        fwd + bwd + (ent[0],) + ent[2:],
    ):
        tab_v[pl.ds(place, 1), :] = row
    tab_v[pl.ds(14, 2), :] = jnp.zeros((2, LANES), jnp.int32)
    table = pltpu.make_async_copy(tab_v, tab_s, loc_sem.at[4])
    table.start()

    for k in range(NB):
        for h in range(C):
            src[h][k] = xb[k, h * ROWS : (h + 1) * ROWS]

    own_w.wait()
    for cp in w_copies:
        cp.wait_recv()
    wfull[...] = jnp.transpose(wt[...].astype(jnp.float32)).astype(jnp.bfloat16)

    table.wait()
    load_t.wait()

    def tile_pass(source, perm, other, keep, contract):
        def body(i, run):
            for u in range(UNROLL):
                t = i * UNROLL + u
                part = lax.dot_general(
                    source[tab_s[other, t]],
                    tv[tab_s[perm, t]],
                    (((1,), (contract,)), ((), ())),
                    preferred_element_type=jnp.float32,
                )
                run = run * tab_s[keep, t].astype(jnp.float32) + part
                buf[t] = run
            return run

        lax.fori_loop(0, T // UNROLL, body, jnp.zeros((ROWS, LANES), jnp.float32))

    def segment(values, last, has, k):
        return values[tab_s[last, k]] * tab_s[has, k].astype(jnp.float32)

    a2a, a2a_own = [], []
    for h in range(C):
        for b in order:
            halo[h, b].wait_recv()
        tile_pass(src[h], F_PERM, F_SRC, F_KEEP, 1)
        for k in range(NB):
            aggS[h, k // NBQ, :, (k % NBQ) * LANES : (k % NBQ + 1) * LANES] = segment(
                buf, F_LAST, F_HAS, k
            ).astype(jnp.bfloat16)
        place = pl.ds(pl.multiple_of(me * FR + h * ROWS, 16), ROWS)
        for d in range(1, F):
            q = feat_peer(d)
            cp = pltpu.make_async_remote_copy(
                src_ref=aggS.at[h, q],
                dst_ref=aggG.at[place, :],
                send_sem=a2a_sem.at[0, h * F + d],
                recv_sem=a2a_sem.at[1, h * F + d],
                device_id=(dom, q),
                device_id_type=MESH,
            )
            cp.start()
            a2a.append(cp)
        cp = pltpu.make_async_copy(aggS.at[h, me], aggG.at[place, :], loc_sem.at[5 + h])
        cp.start()
        a2a_own.append(cp)

    own_cot.wait()
    for cp in cot_copies:
        cp.wait_recv()
    for cp in a2a_own:
        cp.wait()
    for cp in a2a:
        cp.wait_recv()

    def dense(q, c):
        here = pl.ds(pl.multiple_of(q * FR, 16), FR)
        pre = jnp.dot(wt[here, :], aggG[...], preferred_element_type=jnp.float32)
        square = pre * pre
        t = jnp.tanh(GELU_C * pre * (1.0 + GELU_A * square))
        half = 0.5 * (1.0 + t)
        actS[q] = (pre * half).astype(jnp.bfloat16)
        slope = half + (0.5 * GELU_C) * pre * (1.0 - t * t) * (1.0 + (3.0 * GELU_A) * square)
        pg[here, :] = (cotG[here, :].astype(jnp.float32) * slope).astype(jnp.bfloat16)
        return c

    lax.fori_loop(0, F, dense, 0)

    ag, ag_own = [], []
    for h in range(C):

        def agg_grad(q, c, h=h):
            here = pl.ds(pl.multiple_of(q * FR + h * ROWS, 16), ROWS)
            g = jnp.dot(wfull[here, :], pg[...], preferred_element_type=jnp.float32).astype(jnp.bfloat16)
            for k in range(NBQ):
                agS[h, q, k] = g[:, k * LANES : (k + 1) * LANES]
            return c

        lax.fori_loop(0, F, agg_grad, 0)
        place = pl.ds(me * NBQ, NBQ)
        for d in range(1, F):
            q = feat_peer(d)
            cp = pltpu.make_async_remote_copy(
                src_ref=agS.at[h, q],
                dst_ref=gb[h].at[place],
                send_sem=ag_sem.at[0, h * F + d],
                recv_sem=ag_sem.at[1, h * F + d],
                device_id=(dom, q),
                device_id_type=MESH,
            )
            cp.start()
            ag.append(cp)
        cp = pltpu.make_async_copy(agS.at[h, me], gb[h].at[place], loc_sem.at[5 + C + h])
        cp.start()
        ag_own.append(cp)

    place = pl.ds(pl.multiple_of(me * NQ, LANES), NQ)
    act = []
    for d in range(1, F):
        q = feat_peer(d)
        cp = pltpu.make_async_remote_copy(
            src_ref=actS.at[q],
            dst_ref=act_hbm.at[:, place],
            send_sem=act_sem.at[0, d],
            recv_sem=act_sem.at[1, d],
            device_id=(dom, q),
            device_id_type=MESH,
        )
        cp.start()
        act.append(cp)
    act_own = pltpu.make_async_copy(actS.at[me], act_hbm.at[:, place], loc_sem.at[5 + 2 * C])
    act_own.start()

    def weight_term(q, c):
        here = pl.ds(pl.multiple_of(q * FR, 16), FR)
        wpS[q] = lax.dot_general(
            pg[here, :], aggG[...], (((1,), (1,)), ((), ())), preferred_element_type=jnp.float32
        )
        return c

    lax.fori_loop(0, F, weight_term, 0)
    wx = []
    for d in range(1, F):
        cp = pltpu.make_async_remote_copy(
            src_ref=wpS.at[feat_peer(d)],
            dst_ref=wxR.at[d],
            send_sem=wx_sem.at[0, d],
            recv_sem=wx_sem.at[1, d],
            device_id=(dom, feat_peer(d)),
            device_id_type=MESH,
        )
        cp.start()
        wx.append(cp)

    def plane_copy(d, from_ref, to_ref, sem):
        mm = lax.rem(m + d, PLANE)
        return pltpu.make_async_remote_copy(
            src_ref=from_ref(mm),
            dst_ref=to_ref.at[m],
            send_sem=sem.at[0, d],
            recv_sem=sem.at[1, d],
            device_id=(dom_at(mm, zi), me),
            device_id_type=MESH,
        )

    def rs_copy(d):
        return plane_copy(d, lambda mm: wR.at[mm], rsR, rs_sem)

    def fin_copy(d):
        return plane_copy(d, lambda mm: finR.at[m], finR, fin_sem)

    def z_copy(d):
        return pltpu.make_async_remote_copy(
            src_ref=zR.at[zi],
            dst_ref=zR.at[zi],
            send_sem=z_sem.at[0, d],
            recv_sem=z_sem.at[1, d],
            device_id=(dom_at(m, lax.rem(zi + d, Z)), me),
            device_id_type=MESH,
        )

    def each(low, high, act_on):
        def body(d, c):
            act_on(d)
            return c

        lax.fori_loop(low, high, body, 0)

    across = H // LANES

    def reduce_feat():
        for cp in wx:
            cp.wait_recv()
        total = wpS[me]
        for d in range(1, F):
            total = total + wxR[d]
        for p in range(PLANE):
            wR[p] = total[8 * (p // across) : 8 * (p // across) + 8, LANES * (p % across) : LANES * (p % across + 1)]
        each(1, PLANE, lambda d: rs_copy(d).start())

    def reduce_plane():
        rsR[m] = wR[m]
        each(1, PLANE, lambda d: rs_copy(d).wait_recv())
        total = rsR[0]
        for p in range(1, PLANE):
            total = total + rsR[p]
        zR[zi] = total
        each(1, Z, lambda d: z_copy(d).start())

    def reduce_z():
        each(1, Z, lambda d: z_copy(d).wait_recv())
        total = zR[0]
        for p in range(1, Z):
            total = total + zR[p]
        finR[m] = total * (float(NODES * D) ** -0.5)
        each(1, PLANE, lambda d: fin_copy(d).start())

    out_w = pltpu.make_async_copy(wgv, wgrad_hbm, in_sem.at[5])

    def finish_weight():
        each(1, PLANE, lambda d: fin_copy(d).wait_recv())
        whole = jnp.concatenate(
            [
                jnp.concatenate([finR[r * across + a] for a in range(across)], axis=1)
                for r in range(FR // 8)
            ],
            axis=0,
        )
        wgv[...] = whole
        out_w.start()

    def ret_copy(h, b):
        return pltpu.make_async_remote_copy(
            src_ref=ret_s.at[h, pl.ds(b * SB, SB)],
            dst_ref=ret_r[h].at[pl.ds(b * SB, SB)],
            send_sem=ret_sem.at[0, h * R + b],
            recv_sem=ret_sem.at[1, h * R + b],
            device_id=(partner(b), me),
            device_id_type=MESH,
        )

    ret = {}
    for h in range(C):
        ag_own[h].wait()
        for cp in ag[h * (F - 1) : (h + 1) * (F - 1)]:
            cp.wait_recv()
        tile_pass(gb[h], B_PERM, B_SRC, B_KEEP, 0)
        for b in order:
            for j in range(SB):
                s = b * SB + j
                ret_s[h, s] = segment(buf, B_LAST, B_HAS, NB + s).astype(jnp.bfloat16)
            ret[h, b] = ret_copy(h, b)
            ret[h, b].start()
        for k in range(NB):
            fgv[h, k] = segment(buf, B_LAST, B_HAS, k)
        if h == 0:
            reduce_feat()
    reduce_plane()

    outs = []
    for h in range(C):
        for b in order:
            ret[h, b].wait_recv()

        def gather_entry(e, run, h=h):
            run = run * tab_s[E_KEEP, e].astype(jnp.float32) + ret_r[h][tab_s[E_PERM, e]].astype(jnp.float32)
            ebuf[e] = run
            return run

        lax.fori_loop(0, HALO, gather_entry, jnp.zeros((ROWS, LANES), jnp.float32))
        for k in range(NB):
            xv[h * ROWS : (h + 1) * ROWS, k * LANES : (k + 1) * LANES] = (
                fgv[h, k] + segment(ebuf, E_LAST, E_HAS, k)
            ).astype(jnp.bfloat16)
        here = pl.ds(h * ROWS, ROWS)
        cp = pltpu.make_async_copy(xv.at[here, :], fg_hbm.at[here, :], loc_sem.at[6 + 2 * C + h])
        cp.start()
        outs.append(cp)
        if h == 0:
            reduce_z()
    finish_weight()

    for cp in outs:
        cp.wait()
    out_w.wait()
    act_own.wait()
    for cp in act:
        cp.wait_recv()
    for cp in list(halo.values()) + w_copies + cot_copies + a2a + ag + act + wx + list(ret.values()):
        cp.wait_send()
    each(1, PLANE, lambda d: rs_copy(d).wait_send())
    each(1, Z, lambda d: z_copy(d).wait_send())
    each(1, PLANE, lambda d: fin_copy(d).wait_send())


def local(D, F, features, weight, cotangent, tile_values, tile_rows, tile_cols, tile_count, send_lists, send_count):
    FR, NODES = features.shape
    H = weight.shape[0]
    T, BLK, _ = tile_values.shape
    NB = NODES // BLK
    _, R, SB = send_lists.shape
    PLANE = min(D, FR * H // 1024)
    Z = D // PLANE
    C = CHUNKS
    ROWS = FR // C
    HALO = R * SB
    NBQ, NQ = NB // F, NODES // F
    cfg = (H, FR, NODES, NB, T, R, SB, D, F, PLANE, Z)
    bf, f32 = jnp.bfloat16, jnp.float32
    V = pltpu.VMEM
    scratch = [
        V((FR, NODES), bf),
        V((NB, FR, BLK), bf),
        V((T, BLK, BLK), bf),
        V((C, HALO, ROWS, BLK), bf),
        V((C, F, ROWS, NQ), bf),
        V((H, NQ), bf),
        V((H, NQ), bf),
        V((H, H), bf),
        V((H, H), bf),
        V((H, NQ), bf),
        V((F, FR, NQ), bf),
        V((C, F, NBQ, ROWS, BLK), bf),
    ]
    scratch += [V((NB + HALO, ROWS, BLK), bf) for _ in range(C)]
    scratch += [V((NB, ROWS, BLK), bf) for _ in range(C)]
    scratch += [V((T, ROWS, BLK), f32), V((C, HALO, ROWS, BLK), bf)]
    scratch += [V((HALO, ROWS, BLK), bf) for _ in range(C)]
    scratch += [
        V((HALO, ROWS, BLK), f32),
        V((C, NB, ROWS, BLK), f32),
        V((F, FR, H), f32),
        V((F, FR, H), f32),
        V((PLANE, 8, LANES), f32),
        V((PLANE, 8, LANES), f32),
        V((Z, 8, LANES), f32),
        V((PLANE, 8, LANES), f32),
        V((FR, H), f32),
        V((16, LANES), jnp.int32),
        pltpu.SMEM((16, LANES), jnp.int32),
        pltpu.SMEM((T,), jnp.int32),
        pltpu.SMEM((T,), jnp.int32),
        pltpu.SMEM((1,), jnp.int32),
        pltpu.SMEM((R, 1, SB), jnp.int32),
        pltpu.SMEM((1, R), jnp.int32),
    ]
    sem = pltpu.SemaphoreType.DMA
    scratch += [
        sem((6,)),
        sem((6 + 3 * C,)),
        sem((2, C * R)),
        sem((2, C * F)),
        sem((2, F)),
        sem((2, F)),
        sem((2, F)),
        sem((2, C * F)),
        sem((2, C * R)),
        sem((2, F)),
        sem((2, PLANE)),
        sem((2, Z)),
        sem((2, PLANE)),
    ]
    any_spec = pl.BlockSpec(memory_space=pl.ANY)
    act, wgrad, fgrad = pl.pallas_call(
        functools.partial(kernel, cfg),
        out_shape=(
            jax.ShapeDtypeStruct((FR, NODES), bf),
            jax.ShapeDtypeStruct((FR, H), f32),
            jax.ShapeDtypeStruct((FR, NODES), bf),
        ),
        in_specs=[any_spec] * 9,
        out_specs=(any_spec,) * 3,
        scratch_shapes=scratch,
        compiler_params=pltpu.CompilerParams(
            collective_id=0, has_side_effects=True, vmem_limit_bytes=VMEM_LIMIT
        ),
    )(
        features,
        weight.T,
        cotangent,
        tile_values,
        tile_rows,
        tile_cols,
        tile_count,
        jnp.transpose(send_lists, (1, 0, 2)),
        send_count,
    )
    return act, wgrad.T, fgrad


def solution(mesh):
    return jax.shard_map(
        functools.partial(local, mesh.shape["dom"], mesh.shape["feat"]),
        mesh=mesh,
        in_specs=(
            P("feat", "dom"),
            P(None, "feat"),
            P("feat", "dom"),
            P("dom", None, None),
            P("dom"),
            P("dom"),
            P("dom"),
            P("dom", None, None),
            P("dom", None),
        ),
        out_specs=(P("feat", "dom"), P(None, "feat"), P("feat", "dom")),
        check_vma=False,
    )
```

```python
import functools

import jax
import jax.numpy as jnp
from jax import lax
from jax.experimental import pallas as pl
from jax.experimental.pallas import tpu as pltpu
from jax.sharding import PartitionSpec as P

MESH = pl.DeviceIdType.MESH
CHUNKS = 2
UNROLL = 8
LANES = 128
VMEM_LIMIT = 63 * 1024 * 1024
GELU_C = 0.7978845608028654
GELU_A = 0.044715
F_PERM, F_SRC, F_KEEP, F_LAST, F_HAS = 0, 1, 2, 3, 4
B_PERM, B_SRC, B_KEEP, B_LAST, B_HAS = 5, 6, 7, 8, 9
E_PERM, E_KEEP, E_LAST, E_HAS = 10, 11, 12, 13


def sorted_order(key_row, other_row):
    shape = (LANES, LANES)
    ii = lax.broadcasted_iota(jnp.int32, shape, 0)
    jj = lax.broadcasted_iota(jnp.int32, shape, 1)
    key_l = jnp.broadcast_to(key_row, shape)
    other_l = jnp.broadcast_to(other_row, shape)
    key_s = jnp.sum(jnp.where(ii == jj, key_l, 0), axis=1, keepdims=True)
    other_s = jnp.sum(jnp.where(ii == jj, other_l, 0), axis=1, keepdims=True)
    same = jnp.where((key_l == key_s) & (jj < ii), 1, 0)
    dup_s = jnp.sum(same, axis=1, keepdims=True)
    rank_s = dup_s + jnp.sum(jnp.where(key_l < key_s, 1, 0), axis=1, keepdims=True)
    place = rank_s == jj
    perm = jnp.sum(jnp.where(place, ii, 0), axis=0, keepdims=True)
    other = jnp.sum(jnp.where(place, other_s, 0), axis=0, keepdims=True)
    keep = jnp.sum(jnp.where(place, jnp.minimum(dup_s, 1), 0), axis=0, keepdims=True)
    last = jnp.sum(jnp.where(key_s <= jj, 1, 0), axis=0, keepdims=True) - 1
    has = jnp.sum(jnp.where(key_s == jj, 1, 0), axis=0, keepdims=True)
    return perm, other, keep, jnp.maximum(last, 0), jnp.minimum(has, 1)


def kernel(
    cfg,
    x_hbm, w_hbm, cot_hbm, tiles_hbm, rows_hbm, cols_hbm, count_hbm, lists_hbm, sc_hbm,
    act_hbm, wgrad_hbm, fg_hbm,
    *scratch,
):
    (H, FR, NODES, NB, T, R, SB, D, F, PLANE, Z) = cfg
    C = CHUNKS
    ROWS = FR // C
    HALO = R * SB
    NBQ = NB // F
    NQ = NODES // F
    refs = list(scratch)

    def take(n):
        out = refs[:n]
        del refs[:n]
        return out

    (xv, xb, tv, snd, aggS, aggG, cotG, wfull, wt, pg, actS, agS) = take(12)
    src = take(C)
    gb = take(C)
    (buf, ret_s) = take(2)
    ret_r = take(C)
    (ebuf, fgv, wpS, wxR, wR, rsR, zR, finR, wgv, tab_v, tab_s) = take(11)
    (rows_s, cols_s, count_s, lists_s, sc_s) = take(5)
    (in_sem, loc_sem, halo_sem, a2a_sem, w_sem, cot_sem, act_sem, ag_sem, ret_sem, wx_sem, rs_sem, z_sem, fin_sem) = take(13)

    dom = lax.axis_index("dom")
    me = lax.axis_index("feat")
    m = lax.rem(dom, PLANE)
    zi = dom // PLANE

    def dom_at(mm, zz):
        return zz * PLANE + mm

    load_x = pltpu.make_async_copy(x_hbm, xv, loc_sem.at[0])
    load_x.start()
    small = []
    for i, (a, b) in enumerate(
        ((lists_hbm, lists_s), (sc_hbm, sc_s), (rows_hbm, rows_s), (cols_hbm, cols_s), (count_hbm, count_s))
    ):
        small.append(pltpu.make_async_copy(a, b, in_sem.at[i]))
        small[-1].start()
    own_cot = pltpu.make_async_copy(
        cot_hbm.at[:, pl.ds(pl.multiple_of(me * NQ, LANES), NQ)],
        cotG.at[pl.ds(pl.multiple_of(me * FR, 16), FR), :],
        loc_sem.at[2],
    )
    own_cot.start()
    own_rows = pl.ds(pl.multiple_of(me * FR, 16), FR)
    own_w = pltpu.make_async_copy(w_hbm, wt.at[own_rows, :], loc_sem.at[3])
    own_w.start()

    barrier = pltpu.get_barrier_semaphore()
    for d in range(1, F):
        pl.semaphore_signal(barrier, inc=1, device_id=(dom, lax.rem(me + d, F)), device_id_type=MESH)

    def hello_plane(d, c):
        pl.semaphore_signal(
            barrier, inc=1, device_id=(dom_at(lax.rem(m + d, PLANE), zi), me), device_id_type=MESH
        )
        return c

    lax.fori_loop(1, PLANE, hello_plane, 0)

    def hello_z(d, c):
        pl.semaphore_signal(
            barrier, inc=1, device_id=(dom_at(m, lax.rem(zi + d, Z)), me), device_id_type=MESH
        )
        return c

    lax.fori_loop(1, Z, hello_z, 0)

    load_x.wait()
    load_t = pltpu.make_async_copy(tiles_hbm, tv, loc_sem.at[1])
    load_t.start()
    for cp in small:
        cp.wait()

    for k in range(NB):
        xb[k] = xv[:, k * LANES : (k + 1) * LANES]
    zero_block = jnp.zeros((FR, LANES), jnp.int32)
    for b in range(R):

        def fill(j, c, b=b):
            live = (zero_block + j < sc_s[0, b]).astype(jnp.float32)
            block = (xb[lists_s[b, 0, j]].astype(jnp.float32) * live).astype(jnp.bfloat16)
            for h in range(C):
                snd[h, b * SB + j] = block[h * ROWS : (h + 1) * ROWS]
            return c

        lax.fori_loop(0, SB, fill, 0, unroll=True)

    pl.semaphore_wait(barrier, (F - 1) + (PLANE - 1) + (Z - 1))

    def halo_copy(h, b):
        return pltpu.make_async_remote_copy(
            src_ref=snd.at[h, pl.ds(b * SB, SB)],
            dst_ref=src[h].at[pl.ds(NB + b * SB, SB)],
            send_sem=halo_sem.at[0, h * R + b],
            recv_sem=halo_sem.at[1, h * R + b],
            device_id=(partner(b), me),
            device_id_type=MESH,
        )

    def partner(b):
        step = 1 << b
        bit = lax.rem(dom // step, 2)
        return dom + step - 2 * step * bit

    def feat_peer(d):
        return lax.rem(me + d, F)

    order = list(range(R))[::-1]
    sends = []
    halo = {}
    for b in order:
        halo[0, b] = halo_copy(0, b)
        halo[0, b].start()
    w_copies, cot_copies = [], []
    for d in range(1, F):
        q = feat_peer(d)
        cp = pltpu.make_async_remote_copy(
            src_ref=w_hbm,
            dst_ref=wt.at[own_rows, :],
            send_sem=w_sem.at[0, d],
            recv_sem=w_sem.at[1, d],
            device_id=(dom, q),
            device_id_type=MESH,
        )
        cp.start()
        w_copies.append(cp)
        cp = pltpu.make_async_remote_copy(
            src_ref=cot_hbm.at[:, pl.ds(pl.multiple_of(q * NQ, LANES), NQ)],
            dst_ref=cotG.at[pl.ds(pl.multiple_of(me * FR, 16), FR), :],
            send_sem=cot_sem.at[0, d],
            recv_sem=cot_sem.at[1, d],
            device_id=(dom, q),
            device_id_type=MESH,
        )
        cp.start()
        cot_copies.append(cp)
    for h in range(1, C):
        for b in order:
            halo[h, b] = halo_copy(h, b)
            halo[h, b].start()

    lane = lax.broadcasted_iota(jnp.int32, (1, LANES), 1)

    def read_tile(t, c):
        r, k = c
        return jnp.where(lane == t, rows_s[t], r), jnp.where(lane == t, cols_s[t], k)

    zero_row = jnp.zeros((1, LANES), jnp.int32)
    rows_v, cols_v = lax.fori_loop(0, T, read_tile, (zero_row, zero_row))

    list_v = zero_row + (LANES - 1)
    for b in range(R):

        def read_entry(j, c, b=b):
            return jnp.where((lane == b * SB + j) & (zero_row + j < sc_s[0, b]), lists_s[b, 0, j], c)

        list_v = lax.fori_loop(0, SB, read_entry, list_v)
    dead = lane >= count_s[0]
    fwd = sorted_order(jnp.where(dead, LANES - 1, rows_v), cols_v)
    bwd = sorted_order(jnp.where(dead, LANES - 1, cols_v), rows_v)
    ent = sorted_order(list_v, list_v)
    for place, row in zip(
        (F_PERM, F_SRC, F_KEEP, F_LAST, F_HAS, B_PERM, B_SRC, B_KEEP, B_LAST, B_HAS, E_PERM, E_KEEP, E_LAST, E_HAS),
        fwd + bwd + (ent[0],) + ent[2:],
    ):
        tab_v[pl.ds(place, 1), :] = row
    tab_v[pl.ds(14, 2), :] = jnp.zeros((2, LANES), jnp.int32)
    table = pltpu.make_async_copy(tab_v, tab_s, loc_sem.at[4])
    table.start()

    for k in range(NB):
        for h in range(C):
            src[h][k] = xb[k, h * ROWS : (h + 1) * ROWS]

    own_w.wait()
    for cp in w_copies:
        cp.wait_recv()
    wfull[...] = jnp.transpose(wt[...].astype(jnp.float32)).astype(jnp.bfloat16)

    table.wait()
    load_t.wait()

    def tile_pass(source, perm, other, keep, contract):
        def body(i, run):
            for u in range(UNROLL):
                t = i * UNROLL + u
                part = lax.dot_general(
                    source[tab_s[other, t]],
                    tv[tab_s[perm, t]],
                    (((1,), (contract,)), ((), ())),
                    preferred_element_type=jnp.float32,
                )
                run = run * tab_s[keep, t].astype(jnp.float32) + part
                buf[t] = run
            return run

        lax.fori_loop(0, T // UNROLL, body, jnp.zeros((ROWS, LANES), jnp.float32))

    def segment(values, last, has, k):
        return values[tab_s[last, k]] * tab_s[has, k].astype(jnp.float32)

    a2a, a2a_own = [], []
    for h in range(C):
        for b in order:
            halo[h, b].wait_recv()
        tile_pass(src[h], F_PERM, F_SRC, F_KEEP, 1)
        for k in range(NB):
            aggS[h, k // NBQ, :, (k % NBQ) * LANES : (k % NBQ + 1) * LANES] = segment(
                buf, F_LAST, F_HAS, k
            ).astype(jnp.bfloat16)
        place = pl.ds(pl.multiple_of(me * FR + h * ROWS, 16), ROWS)
        for d in range(1, F):
            q = feat_peer(d)
            cp = pltpu.make_async_remote_copy(
                src_ref=aggS.at[h, q],
                dst_ref=aggG.at[place, :],
                send_sem=a2a_sem.at[0, h * F + d],
                recv_sem=a2a_sem.at[1, h * F + d],
                device_id=(dom, q),
                device_id_type=MESH,
            )
            cp.start()
            a2a.append(cp)
        cp = pltpu.make_async_copy(aggS.at[h, me], aggG.at[place, :], loc_sem.at[5 + h])
        cp.start()
        a2a_own.append(cp)

    own_cot.wait()
    for cp in cot_copies:
        cp.wait_recv()
    for cp in a2a_own:
        cp.wait()
    for cp in a2a:
        cp.wait_recv()

    for q in range(F):
        here = slice(q * FR, (q + 1) * FR)
        pre = jnp.dot(wt[here, :], aggG[...], preferred_element_type=jnp.float32)
        square = pre * pre
        t = jnp.tanh(GELU_C * pre * (1.0 + GELU_A * square))
        half = 0.5 * (1.0 + t)
        actS[q] = (pre * half).astype(jnp.bfloat16)
        slope = half + (0.5 * GELU_C) * pre * (1.0 - t * t) * (1.0 + (3.0 * GELU_A) * square)
        pg[here, :] = (cotG[here, :].astype(jnp.float32) * slope).astype(jnp.bfloat16)

    def weight_term(q, c):
        here = pl.ds(pl.multiple_of(q * FR, 16), FR)
        wpS[q] = lax.dot_general(
            pg[here, :], aggG[...], (((1,), (1,)), ((), ())), preferred_element_type=jnp.float32
        ).astype(jnp.bfloat16)
        return c

    lax.fori_loop(0, F, weight_term, 0)
    wx = []
    for d in range(1, F):
        cp = pltpu.make_async_remote_copy(
            src_ref=wpS.at[feat_peer(d)],
            dst_ref=wxR.at[d],
            send_sem=wx_sem.at[0, d],
            recv_sem=wx_sem.at[1, d],
            device_id=(dom, feat_peer(d)),
            device_id_type=MESH,
        )
        cp.start()
        wx.append(cp)

    ag, ag_own = [], []
    for h in range(C):
        for q in range(F):
            here = slice(q * FR + h * ROWS, q * FR + (h + 1) * ROWS)
            g = jnp.dot(wfull[here, :], pg[...], preferred_element_type=jnp.float32).astype(jnp.bfloat16)
            for k in range(NBQ):
                agS[h, q, k] = g[:, k * LANES : (k + 1) * LANES]
        place = pl.ds(me * NBQ, NBQ)
        for d in range(1, F):
            q = feat_peer(d)
            cp = pltpu.make_async_remote_copy(
                src_ref=agS.at[h, q],
                dst_ref=gb[h].at[place],
                send_sem=ag_sem.at[0, h * F + d],
                recv_sem=ag_sem.at[1, h * F + d],
                device_id=(dom, q),
                device_id_type=MESH,
            )
            cp.start()
            ag.append(cp)
        cp = pltpu.make_async_copy(agS.at[h, me], gb[h].at[place], loc_sem.at[5 + C + h])
        cp.start()
        ag_own.append(cp)

    place = pl.ds(pl.multiple_of(me * NQ, LANES), NQ)
    act = []
    for d in range(1, F):
        q = feat_peer(d)
        cp = pltpu.make_async_remote_copy(
            src_ref=actS.at[q],
            dst_ref=act_hbm.at[:, place],
            send_sem=act_sem.at[0, d],
            recv_sem=act_sem.at[1, d],
            device_id=(dom, q),
            device_id_type=MESH,
        )
        cp.start()
        act.append(cp)
    act_own = pltpu.make_async_copy(actS.at[me], act_hbm.at[:, place], loc_sem.at[5 + 2 * C])
    act_own.start()

    def plane_copy(d, from_ref, to_ref, sem):
        mm = lax.rem(m + d, PLANE)
        return pltpu.make_async_remote_copy(
            src_ref=from_ref(mm),
            dst_ref=to_ref.at[m],
            send_sem=sem.at[0, d],
            recv_sem=sem.at[1, d],
            device_id=(dom_at(mm, zi), me),
            device_id_type=MESH,
        )

    def rs_copy(d):
        return plane_copy(d, lambda mm: wR.at[mm], rsR, rs_sem)

    def fin_copy(d):
        return plane_copy(d, lambda mm: finR.at[m], finR, fin_sem)

    def z_copy(d):
        return pltpu.make_async_remote_copy(
            src_ref=zR.at[zi],
            dst_ref=zR.at[zi],
            send_sem=z_sem.at[0, d],
            recv_sem=z_sem.at[1, d],
            device_id=(dom_at(m, lax.rem(zi + d, Z)), me),
            device_id_type=MESH,
        )

    rs, zs, fin = [], [], []

    across = H // LANES

    def reduce_feat():
        for cp in wx:
            cp.wait_recv()
        total = wpS[me].astype(jnp.float32)
        for d in range(1, F):
            total = total + wxR[d].astype(jnp.float32)
        for p in range(PLANE):
            wR[p] = total[8 * (p // across) : 8 * (p // across) + 8, LANES * (p % across) : LANES * (p % across + 1)]
        for d in range(1, PLANE):
            rs.append(rs_copy(d))
            rs[-1].start()

    def reduce_plane():
        rsR[m] = wR[m]
        for cp in rs:
            cp.wait_recv()
        total = rsR[0]
        for p in range(1, PLANE):
            total = total + rsR[p]
        zR[zi] = total
        for d in range(1, Z):
            zs.append(z_copy(d))
            zs[-1].start()

    def reduce_z():
        for cp in zs:
            cp.wait_recv()
        total = zR[0]
        for p in range(1, Z):
            total = total + zR[p]
        finR[m] = total * (float(NODES * D) ** -0.5)
        for d in range(1, PLANE):
            fin.append(fin_copy(d))
            fin[-1].start()

    out_w = pltpu.make_async_copy(wgv, wgrad_hbm, in_sem.at[5])

    def finish_weight():
        for cp in fin:
            cp.wait_recv()
        whole = jnp.concatenate(
            [
                jnp.concatenate([finR[r * across + a] for a in range(across)], axis=1)
                for r in range(FR // 8)
            ],
            axis=0,
        )
        wgv[...] = whole
        out_w.start()

    def ret_copy(h, b):
        return pltpu.make_async_remote_copy(
            src_ref=ret_s.at[h, pl.ds(b * SB, SB)],
            dst_ref=ret_r[h].at[pl.ds(b * SB, SB)],
            send_sem=ret_sem.at[0, h * R + b],
            recv_sem=ret_sem.at[1, h * R + b],
            device_id=(partner(b), me),
            device_id_type=MESH,
        )

    ret = {}
    reduce_feat()
    for h in range(C):
        ag_own[h].wait()
        for cp in ag[h * (F - 1) : (h + 1) * (F - 1)]:
            cp.wait_recv()
        tile_pass(gb[h], B_PERM, B_SRC, B_KEEP, 0)
        for b in order:
            for j in range(SB):
                s = b * SB + j
                ret_s[h, s] = segment(buf, B_LAST, B_HAS, NB + s).astype(jnp.bfloat16)
            ret[h, b] = ret_copy(h, b)
            ret[h, b].start()
        for k in range(NB):
            fgv[h, k] = segment(buf, B_LAST, B_HAS, k)
        if h == 0:
            reduce_plane()

    reduce_z()
    outs = []
    for h in range(C):
        for b in order:
            ret[h, b].wait_recv()

        def gather_entry(e, run, h=h):
            run = run * tab_s[E_KEEP, e].astype(jnp.float32) + ret_r[h][tab_s[E_PERM, e]].astype(jnp.float32)
            ebuf[e] = run
            return run

        lax.fori_loop(0, HALO, gather_entry, jnp.zeros((ROWS, LANES), jnp.float32), unroll=8)
        for k in range(NB):
            xv[h * ROWS : (h + 1) * ROWS, k * LANES : (k + 1) * LANES] = (
                fgv[h, k] + segment(ebuf, E_LAST, E_HAS, k)
            ).astype(jnp.bfloat16)
        here = pl.ds(h * ROWS, ROWS)
        cp = pltpu.make_async_copy(xv.at[here, :], fg_hbm.at[here, :], loc_sem.at[6 + 2 * C + h])
        cp.start()
        outs.append(cp)
    finish_weight()

    for cp in outs:
        cp.wait()
    out_w.wait()
    act_own.wait()
    for cp in act:
        cp.wait_recv()
    for cp in list(halo.values()) + w_copies + cot_copies + a2a + ag + act + wx + list(ret.values()) + rs + zs + fin:
        cp.wait_send()


def settle(a, b, c, out_a, out_b, out_c, va, vb, vc, sem):
    held = ((a, va, out_a), (b, vb, out_b), (c, vc, out_c))
    loads = [pltpu.make_async_copy(x, v, sem.at[0, i]) for i, (x, v, _) in enumerate(held)]
    stores = [pltpu.make_async_copy(v, y, sem.at[1, i]) for i, (_, v, y) in enumerate(held)]
    for cp in loads:
        cp.start()
    for load, store in zip(loads, stores):
        load.wait()
        store.start()
    for cp in stores:
        cp.wait()


def local(D, F, features, weight, cotangent, tile_values, tile_rows, tile_cols, tile_count, send_lists, send_count):
    FR, NODES = features.shape
    H = weight.shape[0]
    T, BLK, _ = tile_values.shape
    NB = NODES // BLK
    _, R, SB = send_lists.shape
    PLANE = min(D, FR * H // 1024)
    Z = D // PLANE
    C = CHUNKS
    ROWS = FR // C
    HALO = R * SB
    NBQ, NQ = NB // F, NODES // F
    cfg = (H, FR, NODES, NB, T, R, SB, D, F, PLANE, Z)
    bf, f32 = jnp.bfloat16, jnp.float32
    V = pltpu.VMEM
    scratch = [
        V((FR, NODES), bf),
        V((NB, FR, BLK), bf),
        V((T, BLK, BLK), bf),
        V((C, HALO, ROWS, BLK), bf),
        V((C, F, ROWS, NQ), bf),
        V((H, NQ), bf),
        V((H, NQ), bf),
        V((H, H), bf),
        V((H, H), bf),
        V((H, NQ), bf),
        V((F, FR, NQ), bf),
        V((C, F, NBQ, ROWS, BLK), bf),
    ]
    scratch += [V((NB + HALO, ROWS, BLK), bf) for _ in range(C)]
    scratch += [V((NB, ROWS, BLK), bf) for _ in range(C)]
    scratch += [V((T, ROWS, BLK), f32), V((C, HALO, ROWS, BLK), bf)]
    scratch += [V((HALO, ROWS, BLK), bf) for _ in range(C)]
    scratch += [
        V((HALO, ROWS, BLK), f32),
        V((C, NB, ROWS, BLK), f32),
        V((F, FR, H), bf),
        V((F, FR, H), bf),
        V((PLANE, 8, LANES), f32),
        V((PLANE, 8, LANES), f32),
        V((Z, 8, LANES), f32),
        V((PLANE, 8, LANES), f32),
        V((FR, H), f32),
        V((16, LANES), jnp.int32),
        pltpu.SMEM((16, LANES), jnp.int32),
        pltpu.SMEM((T,), jnp.int32),
        pltpu.SMEM((T,), jnp.int32),
        pltpu.SMEM((1,), jnp.int32),
        pltpu.SMEM((R, 1, SB), jnp.int32),
        pltpu.SMEM((1, R), jnp.int32),
    ]
    sem = pltpu.SemaphoreType.DMA
    scratch += [
        sem((6,)),
        sem((6 + 3 * C,)),
        sem((2, C * R)),
        sem((2, C * F)),
        sem((2, F)),
        sem((2, F)),
        sem((2, F)),
        sem((2, C * F)),
        sem((2, C * R)),
        sem((2, F)),
        sem((2, PLANE)),
        sem((2, Z)),
        sem((2, PLANE)),
    ]
    any_spec = pl.BlockSpec(memory_space=pl.ANY)
    act, wgrad, fgrad = pl.pallas_call(
        functools.partial(kernel, cfg),
        out_shape=(
            jax.ShapeDtypeStruct((FR, NODES), bf),
            jax.ShapeDtypeStruct((FR, H), f32),
            jax.ShapeDtypeStruct((FR, NODES), bf),
        ),
        in_specs=[any_spec] * 9,
        out_specs=(any_spec,) * 3,
        scratch_shapes=scratch,
        compiler_params=pltpu.CompilerParams(
            collective_id=0, has_side_effects=True, vmem_limit_bytes=VMEM_LIMIT
        ),
    )(
        features,
        weight.T,
        cotangent,
        tile_values,
        tile_rows,
        tile_cols,
        tile_count,
        jnp.transpose(send_lists, (1, 0, 2)),
        send_count,
    )
    act, wgrad, fgrad = pl.pallas_call(
        settle,
        out_shape=tuple(jax.ShapeDtypeStruct(a.shape, a.dtype) for a in (act, wgrad, fgrad)),
        in_specs=[any_spec] * 3,
        out_specs=(any_spec,) * 3,
        scratch_shapes=[V((FR, NODES), bf), V((FR, H), f32), V((FR, NODES), bf), sem((2, 3))],
        compiler_params=pltpu.CompilerParams(vmem_limit_bytes=VMEM_LIMIT),
    )(act, wgrad, fgrad)
    return act, wgrad.T, fgrad


def solution(mesh):
    return jax.shard_map(
        functools.partial(local, mesh.shape["dom"], mesh.shape["feat"]),
        mesh=mesh,
        in_specs=(
            P("feat", "dom"),
            P(None, "feat"),
            P("feat", "dom"),
            P("dom", None, None),
            P("dom"),
            P("dom"),
            P("dom"),
            P("dom", None, None),
            P("dom", None),
        ),
        out_specs=(P("feat", "dom"), P(None, "feat"), P("feat", "dom")),
        check_vma=False,
    )
```

```python
import functools

import jax
import jax.numpy as jnp
from jax import lax
from jax.experimental import pallas as pl
from jax.experimental.pallas import tpu as pltpu
from jax.sharding import PartitionSpec as P

MESH = pl.DeviceIdType.MESH
CHUNKS = 2
UNROLL = 48
LANES = 128
VMEM_LIMIT = 63 * 1024 * 1024
GELU_C = 0.7978845608028654
GELU_A = 0.044715
F_PERM, F_SRC, F_KEEP, F_LAST, F_HAS = 0, 1, 2, 3, 4
B_PERM, B_SRC, B_KEEP, B_LAST, B_HAS = 5, 6, 7, 8, 9
E_PERM, E_KEEP, E_LAST, E_HAS = 10, 11, 12, 13


def sorted_order(key_row, other_row):
    shape = (LANES, LANES)
    ii = lax.broadcasted_iota(jnp.int32, shape, 0)
    jj = lax.broadcasted_iota(jnp.int32, shape, 1)
    key_l = jnp.broadcast_to(key_row, shape)
    other_l = jnp.broadcast_to(other_row, shape)
    key_s = jnp.sum(jnp.where(ii == jj, key_l, 0), axis=1, keepdims=True)
    other_s = jnp.sum(jnp.where(ii == jj, other_l, 0), axis=1, keepdims=True)
    same = jnp.where((key_l == key_s) & (jj < ii), 1, 0)
    dup_s = jnp.sum(same, axis=1, keepdims=True)
    rank_s = dup_s + jnp.sum(jnp.where(key_l < key_s, 1, 0), axis=1, keepdims=True)
    place = rank_s == jj
    perm = jnp.sum(jnp.where(place, ii, 0), axis=0, keepdims=True)
    other = jnp.sum(jnp.where(place, other_s, 0), axis=0, keepdims=True)
    keep = jnp.sum(jnp.where(place, jnp.minimum(dup_s, 1), 0), axis=0, keepdims=True)
    last = jnp.sum(jnp.where(key_s <= jj, 1, 0), axis=0, keepdims=True) - 1
    has = jnp.sum(jnp.where(key_s == jj, 1, 0), axis=0, keepdims=True)
    return perm, other, keep, jnp.maximum(last, 0), jnp.minimum(has, 1)


def kernel(
    cfg,
    x_hbm, w_hbm, cot_hbm, tiles_hbm, rows_hbm, cols_hbm, count_hbm, lists_hbm, sc_hbm,
    act_hbm, wgrad_hbm, fg_hbm,
    *scratch,
):
    (H, FR, NODES, NB, T, R, SB, D, F, Y, Z) = cfg
    C = CHUNKS
    ROWS = FR // C
    HALO = R * SB
    HF = FR // 2
    NBQ = NB // F
    NQ = NODES // F
    refs = list(scratch)

    def take(n):
        out = refs[:n]
        del refs[:n]
        return out

    (xv, xb, tv, snd, aggS, aggG, cotG, wfull, wt, pg, actS, agS) = take(12)
    src = take(C)
    gb = take(C)
    (buf, ret_s) = take(2)
    ret_r = take(C)
    (ebuf, fgv, wpS, wxR, yR, zR, wgv, tab_v, tab_s) = take(9)
    (rows_s, cols_s, count_s, lists_s, sc_s) = take(5)
    (in_sem, loc_sem, halo_sem, a2a_sem, w_sem, cot_sem, act_sem, ag_sem, ret_sem, wx_sem, y_sem, z_sem, fin_sem) = take(13)

    dom = lax.axis_index("dom")
    me = lax.axis_index("feat")
    core = lax.rem(dom, 2)
    yi = lax.rem(dom // 2, Y)
    zi = dom // (2 * Y)

    def dom_at(zz, yy, cc):
        return (zz * Y + yy) * 2 + cc

    load_x = pltpu.make_async_copy(x_hbm, xv, loc_sem.at[0])
    load_x.start()
    small = []
    for i, (a, b) in enumerate(
        ((lists_hbm, lists_s), (sc_hbm, sc_s), (rows_hbm, rows_s), (cols_hbm, cols_s), (count_hbm, count_s))
    ):
        small.append(pltpu.make_async_copy(a, b, in_sem.at[i]))
        small[-1].start()
    own_cot = pltpu.make_async_copy(
        cot_hbm.at[:, pl.ds(pl.multiple_of(me * NQ, LANES), NQ)],
        cotG.at[pl.ds(pl.multiple_of(me * FR, 16), FR), :],
        loc_sem.at[2],
    )
    own_cot.start()
    own_rows = pl.ds(pl.multiple_of(me * FR, 16), FR)
    own_w = pltpu.make_async_copy(w_hbm, wt.at[own_rows, :], loc_sem.at[3])
    own_w.start()

    barrier = pltpu.get_barrier_semaphore()
    pairs = [(dx, dc) for dx in range(F) for dc in range(2)][1:]
    for dx, dc in pairs:
        pl.semaphore_signal(
            barrier,
            inc=1,
            device_id=(dom_at(zi, yi, lax.rem(core + dc, 2)), lax.rem(me + dx, F)),
            device_id_type=MESH,
        )
    for d in range(1, Y):
        pl.semaphore_signal(
            barrier, inc=1, device_id=(dom_at(zi, lax.rem(yi + d, Y), core), me), device_id_type=MESH
        )
    for d in range(1, Z):
        pl.semaphore_signal(
            barrier, inc=1, device_id=(dom_at(lax.rem(zi + d, Z), yi, core), me), device_id_type=MESH
        )

    load_x.wait()
    load_t = pltpu.make_async_copy(tiles_hbm, tv, loc_sem.at[1])
    load_t.start()
    for cp in small:
        cp.wait()

    for k in range(NB):
        xb[k] = xv[:, k * LANES : (k + 1) * LANES]
    zero_block = jnp.zeros((FR, LANES), jnp.int32)
    for b in range(R):

        def fill(j, c, b=b):
            live = (zero_block + j < sc_s[0, b]).astype(jnp.float32)
            block = (xb[lists_s[b, 0, j]].astype(jnp.float32) * live).astype(jnp.bfloat16)
            for h in range(C):
                snd[h, b * SB + j] = block[h * ROWS : (h + 1) * ROWS]
            return c

        lax.fori_loop(0, SB, fill, 0, unroll=True)

    pl.semaphore_wait(barrier, len(pairs) + (Y - 1) + (Z - 1))

    def halo_copy(h, b):
        return pltpu.make_async_remote_copy(
            src_ref=snd.at[h, pl.ds(b * SB, SB)],
            dst_ref=src[h].at[pl.ds(NB + b * SB, SB)],
            send_sem=halo_sem.at[0, h * R + b],
            recv_sem=halo_sem.at[1, h * R + b],
            device_id=(partner(b), me),
            device_id_type=MESH,
        )

    def partner(b):
        step = 1 << b
        bit = lax.rem(dom // step, 2)
        return dom + step - 2 * step * bit

    def feat_peer(d):
        return lax.rem(me + d, F)

    order = list(range(R))[::-1]
    sends = []
    halo = {}
    for b in order:
        halo[0, b] = halo_copy(0, b)
        halo[0, b].start()
    w_copies, cot_copies = [], []
    for d in range(1, F):
        q = feat_peer(d)
        cp = pltpu.make_async_remote_copy(
            src_ref=w_hbm,
            dst_ref=wt.at[own_rows, :],
            send_sem=w_sem.at[0, d],
            recv_sem=w_sem.at[1, d],
            device_id=(dom, q),
            device_id_type=MESH,
        )
        cp.start()
        w_copies.append(cp)
        cp = pltpu.make_async_remote_copy(
            src_ref=cot_hbm.at[:, pl.ds(pl.multiple_of(q * NQ, LANES), NQ)],
            dst_ref=cotG.at[pl.ds(pl.multiple_of(me * FR, 16), FR), :],
            send_sem=cot_sem.at[0, d],
            recv_sem=cot_sem.at[1, d],
            device_id=(dom, q),
            device_id_type=MESH,
        )
        cp.start()
        cot_copies.append(cp)
    for h in range(1, C):
        for b in order:
            halo[h, b] = halo_copy(h, b)
            halo[h, b].start()

    lane = lax.broadcasted_iota(jnp.int32, (1, LANES), 1)

    def read_tile(t, c):
        r, k = c
        return jnp.where(lane == t, rows_s[t], r), jnp.where(lane == t, cols_s[t], k)

    zero_row = jnp.zeros((1, LANES), jnp.int32)
    rows_v, cols_v = lax.fori_loop(0, T, read_tile, (zero_row, zero_row))

    list_v = zero_row + (LANES - 1)
    for b in range(R):

        def read_entry(j, c, b=b):
            return jnp.where((lane == b * SB + j) & (zero_row + j < sc_s[0, b]), lists_s[b, 0, j], c)

        list_v = lax.fori_loop(0, SB, read_entry, list_v)
    dead = lane >= count_s[0]
    fwd = sorted_order(jnp.where(dead, LANES - 1, rows_v), cols_v)
    bwd = sorted_order(jnp.where(dead, LANES - 1, cols_v), rows_v)
    ent = sorted_order(list_v, list_v)
    for place, row in zip(
        (F_PERM, F_SRC, F_KEEP, F_LAST, F_HAS, B_PERM, B_SRC, B_KEEP, B_LAST, B_HAS, E_PERM, E_KEEP, E_LAST, E_HAS),
        fwd + bwd + (ent[0],) + ent[2:],
    ):
        tab_v[pl.ds(place, 1), :] = row
    tab_v[pl.ds(14, 2), :] = jnp.zeros((2, LANES), jnp.int32)
    table = pltpu.make_async_copy(tab_v, tab_s, loc_sem.at[4])
    table.start()

    for k in range(NB):
        for h in range(C):
            src[h][k] = xb[k, h * ROWS : (h + 1) * ROWS]

    own_w.wait()
    for cp in w_copies:
        cp.wait_recv()
    wfull[...] = jnp.transpose(wt[...].astype(jnp.float32)).astype(jnp.bfloat16)

    table.wait()
    load_t.wait()

    unroll = UNROLL if T % UNROLL == 0 else T

    def tile_pass(source, perm, other, keep, contract):
        def body(i, run):
            for u in range(unroll):
                t = i * unroll + u
                part = lax.dot_general(
                    source[tab_s[other, t]],
                    tv[tab_s[perm, t]],
                    (((1,), (contract,)), ((), ())),
                    preferred_element_type=jnp.float32,
                )
                run = run * tab_s[keep, t].astype(jnp.float32) + part
                buf[t] = run
            return run

        lax.fori_loop(0, T // unroll, body, jnp.zeros((ROWS, LANES), jnp.float32))

    def segment(values, last, has, k):
        return values[tab_s[last, k]] * tab_s[has, k].astype(jnp.float32)

    a2a, a2a_own = [], []
    for h in range(C):
        for b in order:
            halo[h, b].wait_recv()
        tile_pass(src[h], F_PERM, F_SRC, F_KEEP, 1)
        for k in range(NB):
            aggS[h, k // NBQ, :, (k % NBQ) * LANES : (k % NBQ + 1) * LANES] = segment(
                buf, F_LAST, F_HAS, k
            ).astype(jnp.bfloat16)
        place = pl.ds(pl.multiple_of(me * FR + h * ROWS, 16), ROWS)
        for d in range(1, F):
            q = feat_peer(d)
            cp = pltpu.make_async_remote_copy(
                src_ref=aggS.at[h, q],
                dst_ref=aggG.at[place, :],
                send_sem=a2a_sem.at[0, h * F + d],
                recv_sem=a2a_sem.at[1, h * F + d],
                device_id=(dom, q),
                device_id_type=MESH,
            )
            cp.start()
            a2a.append(cp)
        cp = pltpu.make_async_copy(aggS.at[h, me], aggG.at[place, :], loc_sem.at[5 + h])
        cp.start()
        a2a_own.append(cp)

    own_cot.wait()
    for cp in cot_copies:
        cp.wait_recv()
    for cp in a2a_own:
        cp.wait()
    for cp in a2a:
        cp.wait_recv()

    for q in range(F):
        here = slice(q * FR, (q + 1) * FR)
        pre = jnp.dot(wt[here, :], aggG[...], preferred_element_type=jnp.float32)
        square = pre * pre
        t = jnp.tanh(GELU_C * pre * (1.0 + GELU_A * square))
        half = 0.5 * (1.0 + t)
        actS[q] = (pre * half).astype(jnp.bfloat16)
        slope = half + (0.5 * GELU_C) * pre * (1.0 - t * t) * (1.0 + (3.0 * GELU_A) * square)
        pg[here, :] = (cotG[here, :].astype(jnp.float32) * slope).astype(jnp.bfloat16)

    ag, ag_own = [], []

    def send_agg_grad(h):
        for q in range(F):
            here = slice(q * FR + h * ROWS, q * FR + (h + 1) * ROWS)
            g = jnp.dot(wfull[here, :], pg[...], preferred_element_type=jnp.float32).astype(jnp.bfloat16)
            for k in range(NBQ):
                agS[h, q, k] = g[:, k * LANES : (k + 1) * LANES]
        place = pl.ds(me * NBQ, NBQ)
        for d in range(1, F):
            q = feat_peer(d)
            cp = pltpu.make_async_remote_copy(
                src_ref=agS.at[h, q],
                dst_ref=gb[h].at[place],
                send_sem=ag_sem.at[0, h * F + d],
                recv_sem=ag_sem.at[1, h * F + d],
                device_id=(dom, q),
                device_id_type=MESH,
            )
            cp.start()
            ag.append(cp)
        cp = pltpu.make_async_copy(agS.at[h, me], gb[h].at[place], loc_sem.at[5 + C + h])
        cp.start()
        ag_own.append(cp)

    wx = []

    def send_weight_term():
        def weight_term(q, c):
            here = pl.ds(pl.multiple_of(q * FR, 16), FR)
            wpS[q] = lax.dot_general(
                pg[here, :], aggG[...], (((1,), (1,)), ((), ())), preferred_element_type=jnp.float32
            ).astype(jnp.bfloat16)
            return c

        lax.fori_loop(0, F, weight_term, 0)
        for i, (dx, dc) in enumerate(pairs):
            c2 = lax.rem(core + dc, 2)
            cp = pltpu.make_async_remote_copy(
                src_ref=wpS.at[feat_peer(dx), pl.ds(pl.multiple_of(c2 * HF, 16), HF)],
                dst_ref=wxR.at[i],
                send_sem=wx_sem.at[0, i],
                recv_sem=wx_sem.at[1, i],
                device_id=(dom_at(zi, yi, c2), feat_peer(dx)),
                device_id_type=MESH,
            )
            cp.start()
            wx.append(cp)

    act, act_own = [], []

    def send_activated():
        place = pl.ds(pl.multiple_of(me * NQ, LANES), NQ)
        for d in range(1, F):
            q = feat_peer(d)
            cp = pltpu.make_async_remote_copy(
                src_ref=actS.at[q],
                dst_ref=act_hbm.at[:, place],
                send_sem=act_sem.at[0, d],
                recv_sem=act_sem.at[1, d],
                device_id=(dom, q),
                device_id_type=MESH,
            )
            cp.start()
            act.append(cp)
        own = pltpu.make_async_copy(actS.at[me], act_hbm.at[:, place], loc_sem.at[5 + 2 * C])
        own.start()
        act_own.append(own)

    send_agg_grad(0)
    send_weight_term()
    for h in range(1, C):
        send_agg_grad(h)
    send_activated()

    own_half = pl.ds(pl.multiple_of(core * HF, 16), HF)
    ys, zs, fin = [], [], []

    def reduce_feat():
        for cp in wx:
            cp.wait_recv()
        total = wpS[me, own_half].astype(jnp.float32)
        for i in range(len(pairs)):
            total = total + wxR[i].astype(jnp.float32)
        yR[yi] = total.astype(jnp.bfloat16)
        for d in range(1, Y):
            cp = pltpu.make_async_remote_copy(
                src_ref=yR.at[yi],
                dst_ref=yR.at[yi],
                send_sem=y_sem.at[0, d],
                recv_sem=y_sem.at[1, d],
                device_id=(dom_at(zi, lax.rem(yi + d, Y), core), me),
                device_id_type=MESH,
            )
            cp.start()
            ys.append(cp)

    def reduce_y():
        for cp in ys:
            cp.wait_recv()
        total = yR[0].astype(jnp.float32)
        for p in range(1, Y):
            total = total + yR[p].astype(jnp.float32)
        zR[zi] = total.astype(jnp.bfloat16)
        for d in range(1, Z):
            cp = pltpu.make_async_remote_copy(
                src_ref=zR.at[zi],
                dst_ref=zR.at[zi],
                send_sem=z_sem.at[0, d],
                recv_sem=z_sem.at[1, d],
                device_id=(dom_at(lax.rem(zi + d, Z), yi, core), me),
                device_id_type=MESH,
            )
            cp.start()
            zs.append(cp)

    def reduce_z():
        for cp in zs:
            cp.wait_recv()
        total = zR[0].astype(jnp.float32)
        for p in range(1, Z):
            total = total + zR[p].astype(jnp.float32)
        wgv[own_half, :] = total * (float(NODES * D) ** -0.5)
        cp = pltpu.make_async_remote_copy(
            src_ref=wgv.at[own_half, :],
            dst_ref=wgv.at[own_half, :],
            send_sem=fin_sem.at[0],
            recv_sem=fin_sem.at[1],
            device_id=(dom_at(zi, yi, 1 - core), me),
            device_id_type=MESH,
        )
        cp.start()
        fin.append(cp)

    out_w = pltpu.make_async_copy(wgv, wgrad_hbm, in_sem.at[5])

    def finish_weight():
        for cp in fin:
            cp.wait_recv()
        out_w.start()

    def ret_copy(h, b):
        return pltpu.make_async_remote_copy(
            src_ref=ret_s.at[h, pl.ds(b * SB, SB)],
            dst_ref=ret_r[h].at[pl.ds(b * SB, SB)],
            send_sem=ret_sem.at[0, h * R + b],
            recv_sem=ret_sem.at[1, h * R + b],
            device_id=(partner(b), me),
            device_id_type=MESH,
        )

    ret = {}
    steps = {"wait 0": reduce_feat, "tiles 1": reduce_y, "sent 1": reduce_z}

    def step(name):
        if name in steps:
            steps[name]()

    for h in range(C):
        step(f"wait {h}")
        ag_own[h].wait()
        for cp in ag[h * (F - 1) : (h + 1) * (F - 1)]:
            cp.wait_recv()
        tile_pass(gb[h], B_PERM, B_SRC, B_KEEP, 0)
        step(f"tiles {h}")
        for b in order:
            for j in range(SB):
                s = b * SB + j
                ret_s[h, s] = segment(buf, B_LAST, B_HAS, NB + s).astype(jnp.bfloat16)
            ret[h, b] = ret_copy(h, b)
            ret[h, b].start()
        for k in range(NB):
            fgv[h, k] = segment(buf, B_LAST, B_HAS, k)
        step(f"sent {h}")

    outs = []
    for h in range(C):
        for b in order:
            ret[h, b].wait_recv()

        def gather_entry(e, run, h=h):
            run = run * tab_s[E_KEEP, e].astype(jnp.float32) + ret_r[h][tab_s[E_PERM, e]].astype(jnp.float32)
            ebuf[e] = run
            return run

        lax.fori_loop(0, HALO, gather_entry, jnp.zeros((ROWS, LANES), jnp.float32), unroll=8)
        for k in range(NB):
            xv[h * ROWS : (h + 1) * ROWS, k * LANES : (k + 1) * LANES] = (
                fgv[h, k] + segment(ebuf, E_LAST, E_HAS, k)
            ).astype(jnp.bfloat16)
        here = pl.ds(h * ROWS, ROWS)
        cp = pltpu.make_async_copy(xv.at[here, :], fg_hbm.at[here, :], loc_sem.at[6 + 2 * C + h])
        cp.start()
        outs.append(cp)
        step(f"final {h}")
    finish_weight()

    for cp in outs:
        cp.wait()
    out_w.wait()
    for cp in act_own:
        cp.wait()
    for cp in act:
        cp.wait_recv()
    for cp in list(halo.values()) + w_copies + cot_copies + a2a + ag + act + wx + list(ret.values()) + ys + zs + fin:
        cp.wait_send()


def settle(a, b, c, out_a, out_b, out_c, va, vb, vc, sem):
    held = ((a, va, out_a), (b, vb, out_b), (c, vc, out_c))
    loads = [pltpu.make_async_copy(x, v, sem.at[0, i]) for i, (x, v, _) in enumerate(held)]
    stores = [pltpu.make_async_copy(v, y, sem.at[1, i]) for i, (_, v, y) in enumerate(held)]
    for cp in loads:
        cp.start()
    for load, store in zip(loads, stores):
        load.wait()
        store.start()
    for cp in stores:
        cp.wait()


def local(D, F, features, weight, cotangent, tile_values, tile_rows, tile_cols, tile_count, send_lists, send_count):
    FR, NODES = features.shape
    H = weight.shape[0]
    T, BLK, _ = tile_values.shape
    NB = NODES // BLK
    _, R, SB = send_lists.shape
    Y = 1 << ((R - 1) // 2)
    Z = D // (2 * Y)
    C = CHUNKS
    ROWS = FR // C
    HALO = R * SB
    NBQ, NQ = NB // F, NODES // F
    cfg = (H, FR, NODES, NB, T, R, SB, D, F, Y, Z)
    bf, f32 = jnp.bfloat16, jnp.float32
    V = pltpu.VMEM
    scratch = [
        V((FR, NODES), bf),
        V((NB, FR, BLK), bf),
        V((T, BLK, BLK), bf),
        V((C, HALO, ROWS, BLK), bf),
        V((C, F, ROWS, NQ), bf),
        V((H, NQ), bf),
        V((H, NQ), bf),
        V((H, H), bf),
        V((H, H), bf),
        V((H, NQ), bf),
        V((F, FR, NQ), bf),
        V((C, F, NBQ, ROWS, BLK), bf),
    ]
    scratch += [V((NB + HALO, ROWS, BLK), bf) for _ in range(C)]
    scratch += [V((NB, ROWS, BLK), bf) for _ in range(C)]
    scratch += [V((T, ROWS, BLK), f32), V((C, HALO, ROWS, BLK), bf)]
    scratch += [V((HALO, ROWS, BLK), bf) for _ in range(C)]
    scratch += [
        V((HALO, ROWS, BLK), f32),
        V((C, NB, ROWS, BLK), f32),
        V((F, FR, H), bf),
        V((2 * F, FR // 2, H), bf),
        V((Y, FR // 2, H), bf),
        V((Z, FR // 2, H), bf),
        V((FR, H), f32),
        V((16, LANES), jnp.int32),
        pltpu.SMEM((16, LANES), jnp.int32),
        pltpu.SMEM((T,), jnp.int32),
        pltpu.SMEM((T,), jnp.int32),
        pltpu.SMEM((1,), jnp.int32),
        pltpu.SMEM((R, 1, SB), jnp.int32),
        pltpu.SMEM((1, R), jnp.int32),
    ]
    sem = pltpu.SemaphoreType.DMA
    scratch += [
        sem((6,)),
        sem((6 + 3 * C,)),
        sem((2, C * R)),
        sem((2, C * F)),
        sem((2, F)),
        sem((2, F)),
        sem((2, F)),
        sem((2, C * F)),
        sem((2, C * R)),
        sem((2, 2 * F)),
        sem((2, Y)),
        sem((2, Z)),
        sem((2,)),
    ]
    any_spec = pl.BlockSpec(memory_space=pl.ANY)
    act, wgrad, fgrad = pl.pallas_call(
        functools.partial(kernel, cfg),
        out_shape=(
            jax.ShapeDtypeStruct((FR, NODES), bf),
            jax.ShapeDtypeStruct((FR, H), f32),
            jax.ShapeDtypeStruct((FR, NODES), bf),
        ),
        in_specs=[any_spec] * 9,
        out_specs=(any_spec,) * 3,
        scratch_shapes=scratch,
        compiler_params=pltpu.CompilerParams(
            collective_id=0, has_side_effects=True, vmem_limit_bytes=VMEM_LIMIT
        ),
    )(
        features,
        weight.T,
        cotangent,
        tile_values,
        tile_rows,
        tile_cols,
        tile_count,
        jnp.transpose(send_lists, (1, 0, 2)),
        send_count,
    )
    act, wgrad, fgrad = pl.pallas_call(
        settle,
        out_shape=tuple(jax.ShapeDtypeStruct(a.shape, a.dtype) for a in (act, wgrad, fgrad)),
        in_specs=[any_spec] * 3,
        out_specs=(any_spec,) * 3,
        scratch_shapes=[V((FR, NODES), bf), V((FR, H), f32), V((FR, NODES), bf), sem((2, 3))],
        compiler_params=pltpu.CompilerParams(vmem_limit_bytes=VMEM_LIMIT),
    )(act, wgrad, fgrad)
    return act, wgrad.T, fgrad


def solution(mesh):
    return jax.shard_map(
        functools.partial(local, mesh.shape["dom"], mesh.shape["feat"]),
        mesh=mesh,
        in_specs=(
            P("feat", "dom"),
            P(None, "feat"),
            P("feat", "dom"),
            P("dom", None, None),
            P("dom"),
            P("dom"),
            P("dom"),
            P("dom", None, None),
            P("dom", None),
        ),
        out_specs=(P("feat", "dom"), P(None, "feat"), P("feat", "dom")),
        check_vma=False,
    )
```

```python
import functools

import jax
import jax.numpy as jnp
from jax import lax
from jax.experimental import pallas as pl
from jax.experimental.pallas import tpu as pltpu
from jax.sharding import PartitionSpec as P

MESH = pl.DeviceIdType.MESH
CHUNKS = 2
UNROLL = 48
LANES = 128
VMEM_LIMIT = 63 * 1024 * 1024
GELU_C = 0.7978845608028654
GELU_A = 0.044715
F_PERM, F_SRC, F_KEEP, F_LAST, F_HAS = 0, 1, 2, 3, 4
B_PERM, B_SRC, B_KEEP, B_LAST, B_HAS = 5, 6, 7, 8, 9
E_PERM, E_KEEP, E_LAST, E_HAS = 10, 11, 12, 13


def sorted_order(key_row, other_row):
    shape = (LANES, LANES)
    ii = lax.broadcasted_iota(jnp.int32, shape, 0)
    jj = lax.broadcasted_iota(jnp.int32, shape, 1)
    key_l = jnp.broadcast_to(key_row, shape)
    other_l = jnp.broadcast_to(other_row, shape)
    key_s = jnp.sum(jnp.where(ii == jj, key_l, 0), axis=1, keepdims=True)
    other_s = jnp.sum(jnp.where(ii == jj, other_l, 0), axis=1, keepdims=True)
    same = jnp.where((key_l == key_s) & (jj < ii), 1, 0)
    dup_s = jnp.sum(same, axis=1, keepdims=True)
    rank_s = dup_s + jnp.sum(jnp.where(key_l < key_s, 1, 0), axis=1, keepdims=True)
    place = rank_s == jj
    perm = jnp.sum(jnp.where(place, ii, 0), axis=0, keepdims=True)
    other = jnp.sum(jnp.where(place, other_s, 0), axis=0, keepdims=True)
    keep = jnp.sum(jnp.where(place, jnp.minimum(dup_s, 1), 0), axis=0, keepdims=True)
    last = jnp.sum(jnp.where(key_s <= jj, 1, 0), axis=0, keepdims=True) - 1
    has = jnp.sum(jnp.where(key_s == jj, 1, 0), axis=0, keepdims=True)
    return perm, other, keep, jnp.maximum(last, 0), jnp.minimum(has, 1)


def kernel(
    cfg,
    x_hbm, w_hbm, cot_hbm, tiles_hbm, rows_hbm, cols_hbm, count_hbm, lists_hbm, sc_hbm,
    act_hbm, wgrad_hbm, fg_hbm,
    *scratch,
):
    (H, FR, NODES, NB, T, R, SB, D, F, Y, Z) = cfg
    C = CHUNKS
    ROWS = FR // C
    HALO = R * SB
    HF = FR // 2
    NBQ = NB // F
    NQ = NODES // F
    refs = list(scratch)

    def take(n):
        out = refs[:n]
        del refs[:n]
        return out

    (xv, xb, tv, snd, aggS, aggG, cotG, wfull, wt, pg, actS, agS) = take(12)
    src = take(C)
    gb = take(C)
    (buf, ret_s) = take(2)
    ret_r = take(C)
    (ebuf, fgv, wpS, wxR, yR, zR, wgv, tab_v, tab_s) = take(9)
    (rows_s, cols_s, count_s, lists_s, sc_s) = take(5)
    (in_sem, loc_sem, halo_sem, a2a_sem, w_sem, cot_sem, act_sem, ag_sem, ret_sem, wx_sem, y_sem, z_sem, fin_sem) = take(13)

    dom = lax.axis_index("dom")
    me = lax.axis_index("feat")
    core = lax.rem(dom, 2)
    yi = lax.rem(dom // 2, Y)
    zi = dom // (2 * Y)

    def dom_at(zz, yy, cc):
        return (zz * Y + yy) * 2 + cc

    load_x = pltpu.make_async_copy(x_hbm, xv, loc_sem.at[0])
    load_x.start()
    small = []
    for i, (a, b) in enumerate(
        ((lists_hbm, lists_s), (sc_hbm, sc_s), (rows_hbm, rows_s), (cols_hbm, cols_s), (count_hbm, count_s))
    ):
        small.append(pltpu.make_async_copy(a, b, in_sem.at[i]))
        small[-1].start()
    own_cot = pltpu.make_async_copy(
        cot_hbm.at[:, pl.ds(pl.multiple_of(me * NQ, LANES), NQ)],
        cotG.at[pl.ds(pl.multiple_of(me * FR, 16), FR), :],
        loc_sem.at[2],
    )
    own_cot.start()
    own_rows = pl.ds(pl.multiple_of(me * FR, 16), FR)
    own_w = pltpu.make_async_copy(w_hbm, wt.at[own_rows, :], loc_sem.at[3])
    own_w.start()

    barrier = pltpu.get_barrier_semaphore()
    pairs = [(dx, dc) for dx in range(F) for dc in range(2)][1:]
    for dx, dc in pairs:
        pl.semaphore_signal(
            barrier,
            inc=1,
            device_id=(dom_at(zi, yi, lax.rem(core + dc, 2)), lax.rem(me + dx, F)),
            device_id_type=MESH,
        )
    for d in range(1, Y):
        pl.semaphore_signal(
            barrier, inc=1, device_id=(dom_at(zi, lax.rem(yi + d, Y), core), me), device_id_type=MESH
        )
    for d in range(1, Z):
        pl.semaphore_signal(
            barrier, inc=1, device_id=(dom_at(lax.rem(zi + d, Z), yi, core), me), device_id_type=MESH
        )

    load_x.wait()
    load_t = pltpu.make_async_copy(tiles_hbm, tv, loc_sem.at[1])
    load_t.start()
    for cp in small:
        cp.wait()

    for k in range(NB):
        xb[k] = xv[:, k * LANES : (k + 1) * LANES]
    zero_block = jnp.zeros((FR, LANES), jnp.int32)
    for b in range(R):

        def fill(j, c, b=b):
            live = (zero_block + j < sc_s[0, b]).astype(jnp.float32)
            block = (xb[lists_s[b, 0, j]].astype(jnp.float32) * live).astype(jnp.bfloat16)
            for h in range(C):
                snd[h, b * SB + j] = block[h * ROWS : (h + 1) * ROWS]
            return c

        lax.fori_loop(0, SB, fill, 0, unroll=True)

    pl.semaphore_wait(barrier, len(pairs) + (Y - 1) + (Z - 1))

    def halo_copy(h, b):
        return pltpu.make_async_remote_copy(
            src_ref=snd.at[h, pl.ds(b * SB, SB)],
            dst_ref=src[h].at[pl.ds(NB + b * SB, SB)],
            send_sem=halo_sem.at[0, h * R + b],
            recv_sem=halo_sem.at[1, h * R + b],
            device_id=(partner(b), me),
            device_id_type=MESH,
        )

    def partner(b):
        step = 1 << b
        bit = lax.rem(dom // step, 2)
        return dom + step - 2 * step * bit

    def feat_peer(d):
        return lax.rem(me + d, F)

    order = list(range(R))[::-1]
    sends = []
    halo = {}
    for b in order:
        halo[0, b] = halo_copy(0, b)
        halo[0, b].start()
    w_copies, cot_copies = [], []
    for d in range(1, F):
        q = feat_peer(d)
        cp = pltpu.make_async_remote_copy(
            src_ref=w_hbm,
            dst_ref=wt.at[own_rows, :],
            send_sem=w_sem.at[0, d],
            recv_sem=w_sem.at[1, d],
            device_id=(dom, q),
            device_id_type=MESH,
        )
        cp.start()
        w_copies.append(cp)
        cp = pltpu.make_async_remote_copy(
            src_ref=cot_hbm.at[:, pl.ds(pl.multiple_of(q * NQ, LANES), NQ)],
            dst_ref=cotG.at[pl.ds(pl.multiple_of(me * FR, 16), FR), :],
            send_sem=cot_sem.at[0, d],
            recv_sem=cot_sem.at[1, d],
            device_id=(dom, q),
            device_id_type=MESH,
        )
        cp.start()
        cot_copies.append(cp)
    for h in range(1, C):
        for b in order:
            halo[h, b] = halo_copy(h, b)
            halo[h, b].start()

    lane = lax.broadcasted_iota(jnp.int32, (1, LANES), 1)

    def read_tile(t, c):
        r, k = c
        return jnp.where(lane == t, rows_s[t], r), jnp.where(lane == t, cols_s[t], k)

    zero_row = jnp.zeros((1, LANES), jnp.int32)
    rows_v, cols_v = lax.fori_loop(0, T, read_tile, (zero_row, zero_row))

    list_v = zero_row + (LANES - 1)
    for b in range(R):

        def read_entry(j, c, b=b):
            return jnp.where((lane == b * SB + j) & (zero_row + j < sc_s[0, b]), lists_s[b, 0, j], c)

        list_v = lax.fori_loop(0, SB, read_entry, list_v)
    dead = lane >= count_s[0]
    fwd = sorted_order(jnp.where(dead, LANES - 1, rows_v), cols_v)
    bwd = sorted_order(jnp.where(dead, LANES - 1, cols_v), rows_v)
    ent = sorted_order(list_v, list_v)
    for place, row in zip(
        (F_PERM, F_SRC, F_KEEP, F_LAST, F_HAS, B_PERM, B_SRC, B_KEEP, B_LAST, B_HAS, E_PERM, E_KEEP, E_LAST, E_HAS),
        fwd + bwd + (ent[0],) + ent[2:],
    ):
        tab_v[pl.ds(place, 1), :] = row
    tab_v[pl.ds(14, 2), :] = jnp.zeros((2, LANES), jnp.int32)
    table = pltpu.make_async_copy(tab_v, tab_s, loc_sem.at[4])
    table.start()

    for k in range(NB):
        for h in range(C):
            src[h][k] = xb[k, h * ROWS : (h + 1) * ROWS]

    own_w.wait()
    for cp in w_copies:
        cp.wait_recv()
    wfull[...] = jnp.transpose(wt[...].astype(jnp.float32)).astype(jnp.bfloat16)

    table.wait()
    load_t.wait()

    unroll = UNROLL if T % UNROLL == 0 else T

    def tile_pass(source, perm, other, keep, contract):
        def body(i, run):
            for u in range(unroll):
                t = i * unroll + u
                part = lax.dot_general(
                    source[tab_s[other, t]],
                    tv[tab_s[perm, t]],
                    (((1,), (contract,)), ((), ())),
                    preferred_element_type=jnp.float32,
                )
                run = run * tab_s[keep, t].astype(jnp.float32) + part
                buf[t] = run
            return run

        lax.fori_loop(0, T // unroll, body, jnp.zeros((ROWS, LANES), jnp.float32))

    def segment(values, last, has, k):
        return values[tab_s[last, k]] * tab_s[has, k].astype(jnp.float32)

    a2a, a2a_own = [], []
    for h in range(C):
        for b in order:
            halo[h, b].wait_recv()
        tile_pass(src[h], F_PERM, F_SRC, F_KEEP, 1)
        for k in range(NB):
            aggS[h, k // NBQ, :, (k % NBQ) * LANES : (k % NBQ + 1) * LANES] = segment(
                buf, F_LAST, F_HAS, k
            ).astype(jnp.bfloat16)
        place = pl.ds(pl.multiple_of(me * FR + h * ROWS, 16), ROWS)
        for d in range(1, F):
            q = feat_peer(d)
            cp = pltpu.make_async_remote_copy(
                src_ref=aggS.at[h, q],
                dst_ref=aggG.at[place, :],
                send_sem=a2a_sem.at[0, h * F + d],
                recv_sem=a2a_sem.at[1, h * F + d],
                device_id=(dom, q),
                device_id_type=MESH,
            )
            cp.start()
            a2a.append(cp)
        cp = pltpu.make_async_copy(aggS.at[h, me], aggG.at[place, :], loc_sem.at[5 + h])
        cp.start()
        a2a_own.append(cp)

    own_cot.wait()
    for cp in cot_copies:
        cp.wait_recv()
    for cp in a2a_own:
        cp.wait()
    for cp in a2a:
        cp.wait_recv()

    for q in range(F):
        here = slice(q * FR, (q + 1) * FR)
        pre = jnp.dot(wt[here, :], aggG[...], preferred_element_type=jnp.float32)
        square = pre * pre
        t = jnp.tanh(GELU_C * pre * (1.0 + GELU_A * square))
        half = 0.5 * (1.0 + t)
        actS[q] = (pre * half).astype(jnp.bfloat16)
        slope = half + (0.5 * GELU_C) * pre * (1.0 - t * t) * (1.0 + (3.0 * GELU_A) * square)
        pg[here, :] = (cotG[here, :].astype(jnp.float32) * slope).astype(jnp.bfloat16)

    ag, ag_own = [], []

    def send_agg_grad(h):
        for q in range(F):
            here = slice(q * FR + h * ROWS, q * FR + (h + 1) * ROWS)
            g = jnp.dot(wfull[here, :], pg[...], preferred_element_type=jnp.float32).astype(jnp.bfloat16)
            for k in range(NBQ):
                agS[h, q, k] = g[:, k * LANES : (k + 1) * LANES]
        place = pl.ds(me * NBQ, NBQ)
        for d in range(1, F):
            q = feat_peer(d)
            cp = pltpu.make_async_remote_copy(
                src_ref=agS.at[h, q],
                dst_ref=gb[h].at[place],
                send_sem=ag_sem.at[0, h * F + d],
                recv_sem=ag_sem.at[1, h * F + d],
                device_id=(dom, q),
                device_id_type=MESH,
            )
            cp.start()
            ag.append(cp)
        cp = pltpu.make_async_copy(agS.at[h, me], gb[h].at[place], loc_sem.at[5 + C + h])
        cp.start()
        ag_own.append(cp)

    wx = []

    def send_weight_term():
        def weight_term(q, c):
            here = pl.ds(pl.multiple_of(q * FR, 16), FR)
            wpS[q] = lax.dot_general(
                pg[here, :], aggG[...], (((1,), (1,)), ((), ())), preferred_element_type=jnp.float32
            ).astype(jnp.bfloat16)
            return c

        lax.fori_loop(0, F, weight_term, 0)
        for i, (dx, dc) in enumerate(pairs):
            c2 = lax.rem(core + dc, 2)
            cp = pltpu.make_async_remote_copy(
                src_ref=wpS.at[feat_peer(dx), pl.ds(pl.multiple_of(c2 * HF, 16), HF)],
                dst_ref=wxR.at[i],
                send_sem=wx_sem.at[0, i],
                recv_sem=wx_sem.at[1, i],
                device_id=(dom_at(zi, yi, c2), feat_peer(dx)),
                device_id_type=MESH,
            )
            cp.start()
            wx.append(cp)

    act, act_own = [], []

    def send_activated():
        place = pl.ds(pl.multiple_of(me * NQ, LANES), NQ)
        for d in range(1, F):
            q = feat_peer(d)
            cp = pltpu.make_async_remote_copy(
                src_ref=actS.at[q],
                dst_ref=act_hbm.at[:, place],
                send_sem=act_sem.at[0, d],
                recv_sem=act_sem.at[1, d],
                device_id=(dom, q),
                device_id_type=MESH,
            )
            cp.start()
            act.append(cp)
        own = pltpu.make_async_copy(actS.at[me], act_hbm.at[:, place], loc_sem.at[5 + 2 * C])
        own.start()
        act_own.append(own)

    send_agg_grad(0)
    send_weight_term()
    for h in range(1, C):
        send_agg_grad(h)

    own_half = pl.ds(pl.multiple_of(core * HF, 16), HF)
    ys, zs, fin = [], [], []

    def reduce_feat():
        for cp in wx:
            cp.wait_recv()
        total = wpS[me, own_half].astype(jnp.float32)
        for i in range(len(pairs)):
            total = total + wxR[i].astype(jnp.float32)
        yR[yi] = total.astype(jnp.bfloat16)
        for d in range(1, Y):
            cp = pltpu.make_async_remote_copy(
                src_ref=yR.at[yi],
                dst_ref=yR.at[yi],
                send_sem=y_sem.at[0, d],
                recv_sem=y_sem.at[1, d],
                device_id=(dom_at(zi, lax.rem(yi + d, Y), core), me),
                device_id_type=MESH,
            )
            cp.start()
            ys.append(cp)

    def reduce_y():
        for cp in ys:
            cp.wait_recv()
        total = yR[0].astype(jnp.float32)
        for p in range(1, Y):
            total = total + yR[p].astype(jnp.float32)
        zR[zi] = total.astype(jnp.bfloat16)
        for d in range(1, Z):
            cp = pltpu.make_async_remote_copy(
                src_ref=zR.at[zi],
                dst_ref=zR.at[zi],
                send_sem=z_sem.at[0, d],
                recv_sem=z_sem.at[1, d],
                device_id=(dom_at(lax.rem(zi + d, Z), yi, core), me),
                device_id_type=MESH,
            )
            cp.start()
            zs.append(cp)

    def reduce_z():
        for cp in zs:
            cp.wait_recv()
        total = zR[0].astype(jnp.float32)
        for p in range(1, Z):
            total = total + zR[p].astype(jnp.float32)
        wgv[own_half, :] = total * (float(NODES * D) ** -0.5)
        cp = pltpu.make_async_remote_copy(
            src_ref=wgv.at[own_half, :],
            dst_ref=wgv.at[own_half, :],
            send_sem=fin_sem.at[0],
            recv_sem=fin_sem.at[1],
            device_id=(dom_at(zi, yi, 1 - core), me),
            device_id_type=MESH,
        )
        cp.start()
        fin.append(cp)

    out_w = pltpu.make_async_copy(wgv, wgrad_hbm, in_sem.at[5])

    def finish_weight():
        for cp in fin:
            cp.wait_recv()
        out_w.start()

    def ret_copy(h, b):
        return pltpu.make_async_remote_copy(
            src_ref=ret_s.at[h, pl.ds(b * SB, SB)],
            dst_ref=ret_r[h].at[pl.ds(b * SB, SB)],
            send_sem=ret_sem.at[0, h * R + b],
            recv_sem=ret_sem.at[1, h * R + b],
            device_id=(partner(b), me),
            device_id_type=MESH,
        )

    ret = {}
    steps = {"wait 0": reduce_feat, "tiles 1": reduce_y, "sent 1": reduce_z}

    def step(name):
        if name in steps:
            steps[name]()

    for h in range(C):
        step(f"wait {h}")
        ag_own[h].wait()
        for cp in ag[h * (F - 1) : (h + 1) * (F - 1)]:
            cp.wait_recv()
        tile_pass(gb[h], B_PERM, B_SRC, B_KEEP, 0)
        step(f"tiles {h}")
        for b in order:
            for j in range(SB):
                s = b * SB + j
                ret_s[h, s] = segment(buf, B_LAST, B_HAS, NB + s).astype(jnp.bfloat16)
            ret[h, b] = ret_copy(h, b)
            ret[h, b].start()
        for k in range(NB):
            fgv[h, k] = segment(buf, B_LAST, B_HAS, k)
        if h == C - 1:
            send_activated()
        step(f"sent {h}")

    outs = []
    for h in range(C):
        for b in order:
            ret[h, b].wait_recv()

        def gather_entry(e, run, h=h):
            run = run * tab_s[E_KEEP, e].astype(jnp.float32) + ret_r[h][tab_s[E_PERM, e]].astype(jnp.float32)
            ebuf[e] = run
            return run

        lax.fori_loop(0, HALO, gather_entry, jnp.zeros((ROWS, LANES), jnp.float32), unroll=8)
        for k in range(NB):
            xv[h * ROWS : (h + 1) * ROWS, k * LANES : (k + 1) * LANES] = (
                fgv[h, k] + segment(ebuf, E_LAST, E_HAS, k)
            ).astype(jnp.bfloat16)
        here = pl.ds(h * ROWS, ROWS)
        cp = pltpu.make_async_copy(xv.at[here, :], fg_hbm.at[here, :], loc_sem.at[6 + 2 * C + h])
        cp.start()
        outs.append(cp)
        step(f"final {h}")
    finish_weight()

    for cp in outs:
        cp.wait()
    out_w.wait()
    for cp in act_own:
        cp.wait()
    for cp in act:
        cp.wait_recv()
    for cp in list(halo.values()) + w_copies + cot_copies + a2a + ag + act + wx + list(ret.values()) + ys + zs + fin:
        cp.wait_send()


def settle(a, b, c, out_a, out_b, out_c, va, vb, vc, sem):
    held = ((a, va, out_a), (b, vb, out_b), (c, vc, out_c))
    loads = [pltpu.make_async_copy(x, v, sem.at[0, i]) for i, (x, v, _) in enumerate(held)]
    stores = [pltpu.make_async_copy(v, y, sem.at[1, i]) for i, (_, v, y) in enumerate(held)]
    for cp in loads:
        cp.start()
    for load, store in zip(loads, stores):
        load.wait()
        store.start()
    for cp in stores:
        cp.wait()


def local(D, F, features, weight, cotangent, tile_values, tile_rows, tile_cols, tile_count, send_lists, send_count):
    FR, NODES = features.shape
    H = weight.shape[0]
    T, BLK, _ = tile_values.shape
    NB = NODES // BLK
    _, R, SB = send_lists.shape
    Y = 1 << ((R - 1) // 2)
    Z = D // (2 * Y)
    C = CHUNKS
    ROWS = FR // C
    HALO = R * SB
    NBQ, NQ = NB // F, NODES // F
    cfg = (H, FR, NODES, NB, T, R, SB, D, F, Y, Z)
    bf, f32 = jnp.bfloat16, jnp.float32
    V = pltpu.VMEM
    scratch = [
        V((FR, NODES), bf),
        V((NB, FR, BLK), bf),
        V((T, BLK, BLK), bf),
        V((C, HALO, ROWS, BLK), bf),
        V((C, F, ROWS, NQ), bf),
        V((H, NQ), bf),
        V((H, NQ), bf),
        V((H, H), bf),
        V((H, H), bf),
        V((H, NQ), bf),
        V((F, FR, NQ), bf),
        V((C, F, NBQ, ROWS, BLK), bf),
    ]
    scratch += [V((NB + HALO, ROWS, BLK), bf) for _ in range(C)]
    scratch += [V((NB, ROWS, BLK), bf) for _ in range(C)]
    scratch += [V((T, ROWS, BLK), f32), V((C, HALO, ROWS, BLK), bf)]
    scratch += [V((HALO, ROWS, BLK), bf) for _ in range(C)]
    scratch += [
        V((HALO, ROWS, BLK), f32),
        V((C, NB, ROWS, BLK), f32),
        V((F, FR, H), bf),
        V((2 * F, FR // 2, H), bf),
        V((Y, FR // 2, H), bf),
        V((Z, FR // 2, H), bf),
        V((FR, H), f32),
        V((16, LANES), jnp.int32),
        pltpu.SMEM((16, LANES), jnp.int32),
        pltpu.SMEM((T,), jnp.int32),
        pltpu.SMEM((T,), jnp.int32),
        pltpu.SMEM((1,), jnp.int32),
        pltpu.SMEM((R, 1, SB), jnp.int32),
        pltpu.SMEM((1, R), jnp.int32),
    ]
    sem = pltpu.SemaphoreType.DMA
    scratch += [
        sem((6,)),
        sem((6 + 3 * C,)),
        sem((2, C * R)),
        sem((2, C * F)),
        sem((2, F)),
        sem((2, F)),
        sem((2, F)),
        sem((2, C * F)),
        sem((2, C * R)),
        sem((2, 2 * F)),
        sem((2, Y)),
        sem((2, Z)),
        sem((2,)),
    ]
    any_spec = pl.BlockSpec(memory_space=pl.ANY)
    act, wgrad, fgrad = pl.pallas_call(
        functools.partial(kernel, cfg),
        out_shape=(
            jax.ShapeDtypeStruct((FR, NODES), bf),
            jax.ShapeDtypeStruct((FR, H), f32),
            jax.ShapeDtypeStruct((FR, NODES), bf),
        ),
        in_specs=[any_spec] * 9,
        out_specs=(any_spec,) * 3,
        scratch_shapes=scratch,
        compiler_params=pltpu.CompilerParams(
            collective_id=0, has_side_effects=True, vmem_limit_bytes=VMEM_LIMIT
        ),
    )(
        features,
        weight.T,
        cotangent,
        tile_values,
        tile_rows,
        tile_cols,
        tile_count,
        jnp.transpose(send_lists, (1, 0, 2)),
        send_count,
    )
    act, wgrad, fgrad = pl.pallas_call(
        settle,
        out_shape=tuple(jax.ShapeDtypeStruct(a.shape, a.dtype) for a in (act, wgrad, fgrad)),
        in_specs=[any_spec] * 3,
        out_specs=(any_spec,) * 3,
        scratch_shapes=[V((FR, NODES), bf), V((FR, H), f32), V((FR, NODES), bf), sem((2, 3))],
        compiler_params=pltpu.CompilerParams(vmem_limit_bytes=VMEM_LIMIT),
    )(act, wgrad, fgrad)
    return act, wgrad.T, fgrad


def solution(mesh):
    return jax.shard_map(
        functools.partial(local, mesh.shape["dom"], mesh.shape["feat"]),
        mesh=mesh,
        in_specs=(
            P("feat", "dom"),
            P(None, "feat"),
            P("feat", "dom"),
            P("dom", None, None),
            P("dom"),
            P("dom"),
            P("dom"),
            P("dom", None, None),
            P("dom", None),
        ),
        out_specs=(P("feat", "dom"), P(None, "feat"), P("feat", "dom")),
        check_vma=False,
    )
```

```python
import functools

import jax
import jax.numpy as jnp
from jax import lax
from jax.experimental import pallas as pl
from jax.experimental.pallas import tpu as pltpu
from jax.sharding import PartitionSpec as P

MESH = pl.DeviceIdType.MESH
CHUNKS = 2
UNROLL = 48
LANES = 128
VMEM_LIMIT = 63 * 1024 * 1024
GELU_C = 0.7978845608028654
GELU_A = 0.044715
F_PERM, F_SRC, F_KEEP, F_LAST, F_HAS = 0, 1, 2, 3, 4
B_PERM, B_SRC, B_KEEP, B_LAST, B_HAS = 5, 6, 7, 8, 9
E_PERM, E_KEEP, E_LAST, E_HAS = 10, 11, 12, 13


def sorted_order(key_row, other_row):
    shape = (LANES, LANES)
    ii = lax.broadcasted_iota(jnp.int32, shape, 0)
    jj = lax.broadcasted_iota(jnp.int32, shape, 1)
    key_l = jnp.broadcast_to(key_row, shape)
    other_l = jnp.broadcast_to(other_row, shape)
    key_s = jnp.sum(jnp.where(ii == jj, key_l, 0), axis=1, keepdims=True)
    other_s = jnp.sum(jnp.where(ii == jj, other_l, 0), axis=1, keepdims=True)
    same = jnp.where((key_l == key_s) & (jj < ii), 1, 0)
    dup_s = jnp.sum(same, axis=1, keepdims=True)
    rank_s = dup_s + jnp.sum(jnp.where(key_l < key_s, 1, 0), axis=1, keepdims=True)
    place = rank_s == jj
    perm = jnp.sum(jnp.where(place, ii, 0), axis=0, keepdims=True)
    other = jnp.sum(jnp.where(place, other_s, 0), axis=0, keepdims=True)
    keep = jnp.sum(jnp.where(place, jnp.minimum(dup_s, 1), 0), axis=0, keepdims=True)
    last = jnp.sum(jnp.where(key_s <= jj, 1, 0), axis=0, keepdims=True) - 1
    has = jnp.sum(jnp.where(key_s == jj, 1, 0), axis=0, keepdims=True)
    return perm, other, keep, jnp.maximum(last, 0), jnp.minimum(has, 1)


def kernel(
    cfg,
    x_hbm, w_hbm, cot_hbm, tiles_hbm, rows_hbm, cols_hbm, count_hbm, lists_hbm, sc_hbm,
    act_hbm, wgrad_hbm, fg_hbm,
    *scratch,
):
    (H, FR, NODES, NB, T, R, SB, D, F, Y, Z) = cfg
    C = CHUNKS
    ROWS = FR // C
    HALO = R * SB
    HF = FR // 2
    NBQ = NB // F
    NQ = NODES // F
    refs = list(scratch)

    def take(n):
        out = refs[:n]
        del refs[:n]
        return out

    (xv, xb, tv, snd, aggS, aggG, cotG, wfull, wt, pg, actS, agS) = take(12)
    src = take(C)
    gb = take(C)
    (buf, ret_s) = take(2)
    ret_r = take(C)
    (ebuf, fgv, wpS, wxR, yR, zR, wgv, tab_v, tab_s) = take(9)
    (rows_s, cols_s, count_s, lists_s, sc_s) = take(5)
    (in_sem, loc_sem, halo_sem, a2a_sem, w_sem, cot_sem, act_sem, ag_sem, ret_sem, wx_sem, y_sem, z_sem, fin_sem) = take(13)

    dom = lax.axis_index("dom")
    me = lax.axis_index("feat")
    core = lax.rem(dom, 2)
    yi = lax.rem(dom // 2, Y)
    zi = dom // (2 * Y)

    def dom_at(zz, yy, cc):
        return (zz * Y + yy) * 2 + cc

    load_x = pltpu.make_async_copy(x_hbm, xv, loc_sem.at[0])
    load_x.start()
    small = []
    for i, (a, b) in enumerate(
        ((lists_hbm, lists_s), (sc_hbm, sc_s), (rows_hbm, rows_s), (cols_hbm, cols_s), (count_hbm, count_s))
    ):
        small.append(pltpu.make_async_copy(a, b, in_sem.at[i]))
        small[-1].start()
    own_cot = pltpu.make_async_copy(
        cot_hbm.at[:, pl.ds(pl.multiple_of(me * NQ, LANES), NQ)],
        cotG.at[pl.ds(pl.multiple_of(me * FR, 16), FR), :],
        loc_sem.at[2],
    )
    own_cot.start()
    own_rows = pl.ds(pl.multiple_of(me * FR, 16), FR)
    own_w = pltpu.make_async_copy(w_hbm, wt.at[own_rows, :], loc_sem.at[3])
    own_w.start()

    barrier = pltpu.get_barrier_semaphore()
    pairs = [(dx, dc) for dx in range(F) for dc in range(2)][1:]
    for dx, dc in pairs:
        pl.semaphore_signal(
            barrier,
            inc=1,
            device_id=(dom_at(zi, yi, lax.rem(core + dc, 2)), lax.rem(me + dx, F)),
            device_id_type=MESH,
        )
    for d in range(1, Y):
        pl.semaphore_signal(
            barrier, inc=1, device_id=(dom_at(zi, lax.rem(yi + d, Y), core), me), device_id_type=MESH
        )
    for d in range(1, Z):
        pl.semaphore_signal(
            barrier, inc=1, device_id=(dom_at(lax.rem(zi + d, Z), yi, core), me), device_id_type=MESH
        )

    load_x.wait()
    load_t = pltpu.make_async_copy(tiles_hbm, tv, loc_sem.at[1])
    load_t.start()
    for cp in small:
        cp.wait()

    for k in range(NB):
        xb[k] = xv[:, k * LANES : (k + 1) * LANES]
    zero_block = jnp.zeros((FR, LANES), jnp.int32)
    for b in range(R):

        def fill(j, c, b=b):
            live = (zero_block + j < sc_s[0, b]).astype(jnp.float32)
            block = (xb[lists_s[b, 0, j]].astype(jnp.float32) * live).astype(jnp.bfloat16)
            for h in range(C):
                snd[h, b * SB + j] = block[h * ROWS : (h + 1) * ROWS]
            return c

        lax.fori_loop(0, SB, fill, 0, unroll=True)

    pl.semaphore_wait(barrier, len(pairs) + (Y - 1) + (Z - 1))

    def halo_copy(h, b):
        return pltpu.make_async_remote_copy(
            src_ref=snd.at[h, pl.ds(b * SB, SB)],
            dst_ref=src[h].at[pl.ds(NB + b * SB, SB)],
            send_sem=halo_sem.at[0, h * R + b],
            recv_sem=halo_sem.at[1, h * R + b],
            device_id=(partner(b), me),
            device_id_type=MESH,
        )

    def partner(b):
        step = 1 << b
        bit = lax.rem(dom // step, 2)
        return dom + step - 2 * step * bit

    def feat_peer(d):
        return lax.rem(me + d, F)

    order = list(range(R))[::-1]
    sends = []
    halo = {}
    for b in order:
        halo[0, b] = halo_copy(0, b)
        halo[0, b].start()
    w_copies, cot_copies = [], []
    for d in range(1, F):
        q = feat_peer(d)
        cp = pltpu.make_async_remote_copy(
            src_ref=w_hbm,
            dst_ref=wt.at[own_rows, :],
            send_sem=w_sem.at[0, d],
            recv_sem=w_sem.at[1, d],
            device_id=(dom, q),
            device_id_type=MESH,
        )
        cp.start()
        w_copies.append(cp)
        cp = pltpu.make_async_remote_copy(
            src_ref=cot_hbm.at[:, pl.ds(pl.multiple_of(q * NQ, LANES), NQ)],
            dst_ref=cotG.at[pl.ds(pl.multiple_of(me * FR, 16), FR), :],
            send_sem=cot_sem.at[0, d],
            recv_sem=cot_sem.at[1, d],
            device_id=(dom, q),
            device_id_type=MESH,
        )
        cp.start()
        cot_copies.append(cp)
    for h in range(1, C):
        for b in order:
            halo[h, b] = halo_copy(h, b)
            halo[h, b].start()

    lane = lax.broadcasted_iota(jnp.int32, (1, LANES), 1)

    def read_tile(t, c):
        r, k = c
        return jnp.where(lane == t, rows_s[t], r), jnp.where(lane == t, cols_s[t], k)

    zero_row = jnp.zeros((1, LANES), jnp.int32)
    rows_v, cols_v = lax.fori_loop(0, T, read_tile, (zero_row, zero_row))

    list_v = zero_row + (LANES - 1)
    for b in range(R):

        def read_entry(j, c, b=b):
            return jnp.where((lane == b * SB + j) & (zero_row + j < sc_s[0, b]), lists_s[b, 0, j], c)

        list_v = lax.fori_loop(0, SB, read_entry, list_v)
    dead = lane >= count_s[0]
    fwd = sorted_order(jnp.where(dead, LANES - 1, rows_v), cols_v)
    bwd = sorted_order(jnp.where(dead, LANES - 1, cols_v), rows_v)
    ent = sorted_order(list_v, list_v)
    for place, row in zip(
        (F_PERM, F_SRC, F_KEEP, F_LAST, F_HAS, B_PERM, B_SRC, B_KEEP, B_LAST, B_HAS, E_PERM, E_KEEP, E_LAST, E_HAS),
        fwd + bwd + (ent[0],) + ent[2:],
    ):
        tab_v[pl.ds(place, 1), :] = row
    tab_v[pl.ds(14, 2), :] = jnp.zeros((2, LANES), jnp.int32)
    table = pltpu.make_async_copy(tab_v, tab_s, loc_sem.at[4])
    table.start()

    for k in range(NB):
        for h in range(C):
            src[h][k] = xb[k, h * ROWS : (h + 1) * ROWS]

    own_w.wait()
    for cp in w_copies:
        cp.wait_recv()
    wfull[...] = jnp.transpose(wt[...].astype(jnp.float32)).astype(jnp.bfloat16)

    table.wait()
    load_t.wait()

    unroll = UNROLL if T % UNROLL == 0 else T

    def tile_pass(source, perm, other, keep, contract):
        def body(i, run):
            for u in range(unroll):
                t = i * unroll + u
                part = lax.dot_general(
                    source[tab_s[other, t]],
                    tv[tab_s[perm, t]],
                    (((1,), (contract,)), ((), ())),
                    preferred_element_type=jnp.float32,
                )
                run = run * tab_s[keep, t].astype(jnp.float32) + part
                buf[t] = run
            return run

        lax.fori_loop(0, T // unroll, body, jnp.zeros((ROWS, LANES), jnp.float32))

    def segment(values, last, has, k):
        return values[tab_s[last, k]] * tab_s[has, k].astype(jnp.float32)

    a2a, a2a_own = [], []
    for h in range(C):
        for b in order:
            halo[h, b].wait_recv()
        tile_pass(src[h], F_PERM, F_SRC, F_KEEP, 1)
        for k in range(NB):
            aggS[h, k // NBQ, :, (k % NBQ) * LANES : (k % NBQ + 1) * LANES] = segment(
                buf, F_LAST, F_HAS, k
            ).astype(jnp.bfloat16)
        place = pl.ds(pl.multiple_of(me * FR + h * ROWS, 16), ROWS)
        for d in range(1, F):
            q = feat_peer(d)
            cp = pltpu.make_async_remote_copy(
                src_ref=aggS.at[h, q],
                dst_ref=aggG.at[place, :],
                send_sem=a2a_sem.at[0, h * F + d],
                recv_sem=a2a_sem.at[1, h * F + d],
                device_id=(dom, q),
                device_id_type=MESH,
            )
            cp.start()
            a2a.append(cp)
        cp = pltpu.make_async_copy(aggS.at[h, me], aggG.at[place, :], loc_sem.at[5 + h])
        cp.start()
        a2a_own.append(cp)

    own_cot.wait()
    for cp in cot_copies:
        cp.wait_recv()
    for cp in a2a_own:
        cp.wait()
    for cp in a2a:
        cp.wait_recv()

    for q in range(F):
        here = slice(q * FR, (q + 1) * FR)
        pre = jnp.dot(wt[here, :], aggG[...], preferred_element_type=jnp.float32)
        square = pre * pre
        t = jnp.tanh(GELU_C * pre * (1.0 + GELU_A * square))
        half = 0.5 * (1.0 + t)
        actS[q] = (pre * half).astype(jnp.bfloat16)
        slope = half + (0.5 * GELU_C) * pre * (1.0 - t * t) * (1.0 + (3.0 * GELU_A) * square)
        pg[here, :] = (cotG[here, :].astype(jnp.float32) * slope).astype(jnp.bfloat16)

    ag, ag_own = [], []

    def send_agg_grad(h):
        for q in range(F):
            here = slice(q * FR + h * ROWS, q * FR + (h + 1) * ROWS)
            g = jnp.dot(wfull[here, :], pg[...], preferred_element_type=jnp.float32).astype(jnp.bfloat16)
            for k in range(NBQ):
                agS[h, q, k] = g[:, k * LANES : (k + 1) * LANES]
        place = pl.ds(me * NBQ, NBQ)
        for d in range(1, F):
            q = feat_peer(d)
            cp = pltpu.make_async_remote_copy(
                src_ref=agS.at[h, q],
                dst_ref=gb[h].at[place],
                send_sem=ag_sem.at[0, h * F + d],
                recv_sem=ag_sem.at[1, h * F + d],
                device_id=(dom, q),
                device_id_type=MESH,
            )
            cp.start()
            ag.append(cp)
        cp = pltpu.make_async_copy(agS.at[h, me], gb[h].at[place], loc_sem.at[5 + C + h])
        cp.start()
        ag_own.append(cp)

    wx = []

    def send_weight_term():
        def weight_term(q, c):
            here = pl.ds(pl.multiple_of(q * FR, 16), FR)
            wpS[q] = lax.dot_general(
                pg[here, :], aggG[...], (((1,), (1,)), ((), ())), preferred_element_type=jnp.float32
            ).astype(jnp.bfloat16)
            return c

        lax.fori_loop(0, F, weight_term, 0, unroll=True)
        for i, (dx, dc) in enumerate(pairs):
            c2 = lax.rem(core + dc, 2)
            cp = pltpu.make_async_remote_copy(
                src_ref=wpS.at[feat_peer(dx), pl.ds(pl.multiple_of(c2 * HF, 16), HF)],
                dst_ref=wxR.at[i],
                send_sem=wx_sem.at[0, i],
                recv_sem=wx_sem.at[1, i],
                device_id=(dom_at(zi, yi, c2), feat_peer(dx)),
                device_id_type=MESH,
            )
            cp.start()
            wx.append(cp)

    act, act_own = [], []

    def send_activated():
        place = pl.ds(pl.multiple_of(me * NQ, LANES), NQ)
        for d in range(1, F):
            q = feat_peer(d)
            cp = pltpu.make_async_remote_copy(
                src_ref=actS.at[q],
                dst_ref=act_hbm.at[:, place],
                send_sem=act_sem.at[0, d],
                recv_sem=act_sem.at[1, d],
                device_id=(dom, q),
                device_id_type=MESH,
            )
            cp.start()
            act.append(cp)
        own = pltpu.make_async_copy(actS.at[me], act_hbm.at[:, place], loc_sem.at[5 + 2 * C])
        own.start()
        act_own.append(own)

    send_agg_grad(0)
    send_weight_term()
    for h in range(1, C):
        send_agg_grad(h)

    own_half = pl.ds(pl.multiple_of(core * HF, 16), HF)
    ys, zs, fin = [], [], []

    def reduce_feat():
        for cp in wx:
            cp.wait_recv()
        total = wpS[me, own_half].astype(jnp.float32)
        for i in range(len(pairs)):
            total = total + wxR[i].astype(jnp.float32)
        yR[yi] = total.astype(jnp.bfloat16)
        for d in range(1, Y):
            cp = pltpu.make_async_remote_copy(
                src_ref=yR.at[yi],
                dst_ref=yR.at[yi],
                send_sem=y_sem.at[0, d],
                recv_sem=y_sem.at[1, d],
                device_id=(dom_at(zi, lax.rem(yi + d, Y), core), me),
                device_id_type=MESH,
            )
            cp.start()
            ys.append(cp)

    def reduce_y():
        for cp in ys:
            cp.wait_recv()
        total = yR[0].astype(jnp.float32)
        for p in range(1, Y):
            total = total + yR[p].astype(jnp.float32)
        zR[zi] = total.astype(jnp.bfloat16)
        for d in range(1, Z):
            cp = pltpu.make_async_remote_copy(
                src_ref=zR.at[zi],
                dst_ref=zR.at[zi],
                send_sem=z_sem.at[0, d],
                recv_sem=z_sem.at[1, d],
                device_id=(dom_at(lax.rem(zi + d, Z), yi, core), me),
                device_id_type=MESH,
            )
            cp.start()
            zs.append(cp)

    def reduce_z():
        for cp in zs:
            cp.wait_recv()
        total = zR[0].astype(jnp.float32)
        for p in range(1, Z):
            total = total + zR[p].astype(jnp.float32)
        wgv[own_half, :] = total * (float(NODES * D) ** -0.5)
        cp = pltpu.make_async_remote_copy(
            src_ref=wgv.at[own_half, :],
            dst_ref=wgv.at[own_half, :],
            send_sem=fin_sem.at[0],
            recv_sem=fin_sem.at[1],
            device_id=(dom_at(zi, yi, 1 - core), me),
            device_id_type=MESH,
        )
        cp.start()
        fin.append(cp)

    out_w = pltpu.make_async_copy(wgv, wgrad_hbm, in_sem.at[5])

    def finish_weight():
        for cp in fin:
            cp.wait_recv()
        out_w.start()

    def ret_copy(h, b):
        return pltpu.make_async_remote_copy(
            src_ref=ret_s.at[h, pl.ds(b * SB, SB)],
            dst_ref=ret_r[h].at[pl.ds(b * SB, SB)],
            send_sem=ret_sem.at[0, h * R + b],
            recv_sem=ret_sem.at[1, h * R + b],
            device_id=(partner(b), me),
            device_id_type=MESH,
        )

    ret = {}
    steps = {"wait 0": reduce_feat, "tiles 1": reduce_y, "sent 1": reduce_z}

    def step(name):
        if name in steps:
            steps[name]()

    for h in range(C):
        step(f"wait {h}")
        ag_own[h].wait()
        for cp in ag[h * (F - 1) : (h + 1) * (F - 1)]:
            cp.wait_recv()
        tile_pass(gb[h], B_PERM, B_SRC, B_KEEP, 0)
        step(f"tiles {h}")
        for b in order:
            for j in range(SB):
                s = b * SB + j
                ret_s[h, s] = segment(buf, B_LAST, B_HAS, NB + s).astype(jnp.bfloat16)
            ret[h, b] = ret_copy(h, b)
            ret[h, b].start()
        for k in range(NB):
            fgv[h, k] = segment(buf, B_LAST, B_HAS, k)
        if h == C - 1:
            send_activated()
        step(f"sent {h}")

    outs = []
    for h in range(C):
        for b in order:
            ret[h, b].wait_recv()

        def gather_entry(e, run, h=h):
            run = run * tab_s[E_KEEP, e].astype(jnp.float32) + ret_r[h][tab_s[E_PERM, e]].astype(jnp.float32)
            ebuf[e] = run
            return run

        lax.fori_loop(0, HALO, gather_entry, jnp.zeros((ROWS, LANES), jnp.float32), unroll=8)
        for k in range(NB):
            xv[h * ROWS : (h + 1) * ROWS, k * LANES : (k + 1) * LANES] = (
                fgv[h, k] + segment(ebuf, E_LAST, E_HAS, k)
            ).astype(jnp.bfloat16)
        here = pl.ds(h * ROWS, ROWS)
        cp = pltpu.make_async_copy(xv.at[here, :], fg_hbm.at[here, :], loc_sem.at[6 + 2 * C + h])
        cp.start()
        outs.append(cp)
        step(f"final {h}")
    finish_weight()

    for cp in outs:
        cp.wait()
    out_w.wait()
    for cp in act_own:
        cp.wait()
    for cp in act:
        cp.wait_recv()
    for cp in list(halo.values()) + w_copies + cot_copies + a2a + ag + act + wx + list(ret.values()) + ys + zs + fin:
        cp.wait_send()


def settle(a, b, c, out_a, out_b, out_c, va, vb, vc, sem):
    held = ((a, va, out_a), (b, vb, out_b), (c, vc, out_c))
    loads = [pltpu.make_async_copy(x, v, sem.at[0, i]) for i, (x, v, _) in enumerate(held)]
    stores = [pltpu.make_async_copy(v, y, sem.at[1, i]) for i, (_, v, y) in enumerate(held)]
    for cp in loads:
        cp.start()
    for load, store in zip(loads, stores):
        load.wait()
        store.start()
    for cp in stores:
        cp.wait()


def local(D, F, features, weight, cotangent, tile_values, tile_rows, tile_cols, tile_count, send_lists, send_count):
    FR, NODES = features.shape
    H = weight.shape[0]
    T, BLK, _ = tile_values.shape
    NB = NODES // BLK
    _, R, SB = send_lists.shape
    Y = 1 << ((R - 1) // 2)
    Z = D // (2 * Y)
    C = CHUNKS
    ROWS = FR // C
    HALO = R * SB
    NBQ, NQ = NB // F, NODES // F
    cfg = (H, FR, NODES, NB, T, R, SB, D, F, Y, Z)
    bf, f32 = jnp.bfloat16, jnp.float32
    V = pltpu.VMEM
    scratch = [
        V((FR, NODES), bf),
        V((NB, FR, BLK), bf),
        V((T, BLK, BLK), bf),
        V((C, HALO, ROWS, BLK), bf),
        V((C, F, ROWS, NQ), bf),
        V((H, NQ), bf),
        V((H, NQ), bf),
        V((H, H), bf),
        V((H, H), bf),
        V((H, NQ), bf),
        V((F, FR, NQ), bf),
        V((C, F, NBQ, ROWS, BLK), bf),
    ]
    scratch += [V((NB + HALO, ROWS, BLK), bf) for _ in range(C)]
    scratch += [V((NB, ROWS, BLK), bf) for _ in range(C)]
    scratch += [V((T, ROWS, BLK), f32), V((C, HALO, ROWS, BLK), bf)]
    scratch += [V((HALO, ROWS, BLK), bf) for _ in range(C)]
    scratch += [
        V((HALO, ROWS, BLK), f32),
        V((C, NB, ROWS, BLK), f32),
        V((F, FR, H), bf),
        V((2 * F, FR // 2, H), bf),
        V((Y, FR // 2, H), bf),
        V((Z, FR // 2, H), bf),
        V((FR, H), f32),
        V((16, LANES), jnp.int32),
        pltpu.SMEM((16, LANES), jnp.int32),
        pltpu.SMEM((T,), jnp.int32),
        pltpu.SMEM((T,), jnp.int32),
        pltpu.SMEM((1,), jnp.int32),
        pltpu.SMEM((R, 1, SB), jnp.int32),
        pltpu.SMEM((1, R), jnp.int32),
    ]
    sem = pltpu.SemaphoreType.DMA
    scratch += [
        sem((6,)),
        sem((6 + 3 * C,)),
        sem((2, C * R)),
        sem((2, C * F)),
        sem((2, F)),
        sem((2, F)),
        sem((2, F)),
        sem((2, C * F)),
        sem((2, C * R)),
        sem((2, 2 * F)),
        sem((2, Y)),
        sem((2, Z)),
        sem((2,)),
    ]
    any_spec = pl.BlockSpec(memory_space=pl.ANY)
    act, wgrad, fgrad = pl.pallas_call(
        functools.partial(kernel, cfg),
        out_shape=(
            jax.ShapeDtypeStruct((FR, NODES), bf),
            jax.ShapeDtypeStruct((FR, H), f32),
            jax.ShapeDtypeStruct((FR, NODES), bf),
        ),
        in_specs=[any_spec] * 9,
        out_specs=(any_spec,) * 3,
        scratch_shapes=scratch,
        compiler_params=pltpu.CompilerParams(
            collective_id=0, has_side_effects=True, vmem_limit_bytes=VMEM_LIMIT
        ),
    )(
        features,
        weight.T,
        cotangent,
        tile_values,
        tile_rows,
        tile_cols,
        tile_count,
        jnp.transpose(send_lists, (1, 0, 2)),
        send_count,
    )
    act, wgrad, fgrad = pl.pallas_call(
        settle,
        out_shape=tuple(jax.ShapeDtypeStruct(a.shape, a.dtype) for a in (act, wgrad, fgrad)),
        in_specs=[any_spec] * 3,
        out_specs=(any_spec,) * 3,
        scratch_shapes=[V((FR, NODES), bf), V((FR, H), f32), V((FR, NODES), bf), sem((2, 3))],
        compiler_params=pltpu.CompilerParams(vmem_limit_bytes=VMEM_LIMIT),
    )(act, wgrad, fgrad)
    return act, wgrad.T, fgrad


def solution(mesh):
    return jax.shard_map(
        functools.partial(local, mesh.shape["dom"], mesh.shape["feat"]),
        mesh=mesh,
        in_specs=(
            P("feat", "dom"),
            P(None, "feat"),
            P("feat", "dom"),
            P("dom", None, None),
            P("dom"),
            P("dom"),
            P("dom"),
            P("dom", None, None),
            P("dom", None),
        ),
        out_specs=(P("feat", "dom"), P(None, "feat"), P("feat", "dom")),
        check_vma=False,
    )
```
